512 devices in a mesh: ctx: 64 (over z, x, core), head: 8 (over y).
Axes of the slice: x: 4, y: 8, z: 8, core: 2. Of those that a mesh axis runs over, the one named last changes fastest.
Arguments:
- hidden: bfloat16 [65536, 2048], P('ctx'), may hold values from -16 to 16
- qkv_weight: bfloat16 [2048, 3072], P('ctx', 'head'), may hold values from -0.125 to 0.125
- out_grad: float32 [65536, 1024], P('ctx', 'head'), may hold values from -6 to 6
Outputs:
- attended: float32 [65536, 1024], P('ctx', 'head')
- weight_grad: float32 [2048, 3072], P('ctx', 'head')
The draws below stay inside these ranges and needn't reach their ends.
All inputs are finite; a program needn't handle non-finite values.
Results may differ from the reference program's by a relative error of at most 0.0018.
Values may be sent and summed in bfloat16 or wider, within the bound.
No kernel may reach another device: no remote copies, remote signals or barrier semaphores. Data moves between devices by JAX's collectives and lax.ppermute only.
A program may use at most 64 MiB of HBM per device.

```python
import jax
import jax.numpy as jnp
from jax import lax

D = 2048
H = 8
HD = 128
BLOCK = 128
SEQ = 65536


def strengthened(entries, rng, source, target, shards_of, factor):
    owner, partner = [(jnp.arange(entries.shape[position]) // (entries.shape[position] // shards_of)).reshape([-1 if axis == position else 1 for axis in range(entries.ndim)]) for position in (source, target)]
    chosen = jax.random.permutation(rng, shards_of)[partner]
    strong = (owner == chosen) | (owner == (partner + shards_of // 2) % shards_of)
    return jnp.where(strong, factor * entries, entries)


def block_scale(own_key, shape, shards, least, high):
    factor_of = 1.0
    for position, shards_of in shards:
        steps = jax.random.uniform(jax.random.fold_in(jax.random.fold_in(own_key, 6), position), (shards_of,), jnp.float32, least / len(shards), high / len(shards))
        factor_of = factor_of * jnp.repeat(jnp.exp(steps), shape[position] // shards_of).reshape((-1,) + (1,) * (len(shape) - 1 - position))
    return factor_of


def noise(key, dims, deviation, limit, pieces=(), dtype=jnp.bfloat16):
    entries = deviation * jax.random.normal(key, dims, jnp.float32)
    if pieces:
        entries = entries * block_scale(key, dims, pieces, -0.22, 0.18)
    return jnp.clip(entries, -limit, limit).astype(dtype)


def bell_draw_with(stream_key, dims, width, bound, pieces, heavy, dtype=jnp.bfloat16):
    entries = width * jax.random.normal(stream_key, dims, jnp.float32)
    if pieces:
        entries = entries * block_scale(stream_key, dims, pieces, -0.22, 0.18)
    return jnp.clip(strengthened(entries, jax.random.fold_in(stream_key, 3), *heavy), -bound, bound).astype(dtype)


def setup_inputs(seed: int = 0) -> dict:
    splits = jax.random.split(jax.random.key(seed), 4)
    return {
        "hidden": bell_draw_with(splits[0], (SEQ, D), 1.0, 16.0, ((0, 64),), (0, 1, 64, 4.0)),
        "qkv_weight": noise(splits[1], (D, 3 * H * HD), D ** -0.5, 0.125, ((0, 64), (1, 8))),
        "out_grad": noise(splits[2], (SEQ, H * HD), 1.0, 6.0, ((0, 64), (1, 8)), jnp.float32),
    }


HIGH = lax.Precision.HIGHEST

def attend(q, k, v, scale):
    count = q.shape[0] // BLOCK
    qb = q.reshape(count, BLOCK, H, HD)
    kb = k.reshape(count, BLOCK, H, HD)
    vb = v.reshape(count, BLOCK, H, HD)
    rows = jnp.arange(BLOCK)
    mask = (rows[:, None] >= rows[None, :]).astype(jnp.float32)
    scores = jnp.einsum('nthd,nshd->nhts', qb, kb, precision=HIGH) * mask
    inner = jnp.einsum('nhts,nshe->nthe', scores, vb, precision=HIGH)
    states = jnp.einsum('nshd,nshe->nhde', kb, vb, precision=HIGH)
    before = jnp.cumsum(states, axis=0) - states
    carried = jnp.einsum('nthd,nhde->nthe', qb, before, precision=HIGH)
    return (scale * (inner + carried)).reshape(q.shape[0], H * HD)

def reference(hidden, qkv_weight, out_grad):
    scale = float(HD * SEQ) ** (-0.5)
    proj = jnp.dot(hidden, qkv_weight, preferred_element_type=jnp.float32)

    def forward(flat):
        parts = flat.reshape(SEQ, H, 3, HD)
        return attend(parts[:, :, 0], parts[:, :, 1], parts[:, :, 2], scale)
    attended, pullback = jax.vjp(forward, proj)
    dproj, = pullback(out_grad)
    dproj = dproj.astype(jnp.bfloat16)
    grad = jnp.dot(hidden.T, dproj, preferred_element_type=jnp.float32)
    return (attended, grad * float(SEQ) ** (-0.5))
```

```python
import jax
import jax.numpy as jnp
from jax import lax
from jax.sharding import Mesh, PartitionSpec as P

HD = 128
BLOCK = 128
CORES = 2

HIGH = lax.Precision.HIGH
HIGHEST = lax.Precision.HIGHEST
SWAP = [(0, 1), (1, 0)]
CTX = ("chip", "core")


def gathered_weight(weight):
    chips = lax.axis_size("chip")
    core = lax.axis_index("core")
    spread = jnp.broadcast_to(weight[None], (chips,) + weight.shape)
    mine = lax.all_to_all(spread, "chip", 0, 0, tiled=True)
    other = lax.ppermute(mine, "core", SWAP)
    first = jnp.where(core == 0, mine, other)
    second = jnp.where(core == 0, other, mine)
    whole = jnp.stack([first, second], axis=1)
    return whole.reshape(-1, weight.shape[1])


def exchanged_states(kv_total, qg_total):
    chips = lax.axis_size("chip")
    devices = chips * CORES
    core = lax.axis_index("core")
    rows = HD // chips
    parts = jnp.stack(
        [kv_total.reshape(chips, rows, HD), qg_total.reshape(chips, rows, HD)], axis=1
    ).reshape(devices, rows, HD)
    pieces = lax.all_to_all(parts, CTX, 0, 0, tiled=True)
    place = jnp.arange(devices)
    earlier = place[:, None] > place[None, :]
    chosen = jnp.where(core == 0, earlier, earlier.T).astype(jnp.float32)
    sums = jnp.dot(chosen, pieces.reshape(devices, rows * HD), precision=HIGHEST)
    back = lax.all_to_all(sums.reshape(devices, rows, HD), CTX, 0, 0, tiled=True)
    back = back.reshape(chips, CORES, rows, HD)
    return back[:, 0].reshape(HD, HD), back[:, 1].reshape(HD, HD)


def summed_gradient(product):
    chips = lax.axis_size("chip")
    core = lax.axis_index("core")
    rows = product.shape[0] // (chips * CORES)
    halves = product.reshape(chips, CORES, rows, product.shape[1])
    keep = jnp.where(core == 0, halves[:, 0], halves[:, 1])
    give = jnp.where(core == 0, halves[:, 1], halves[:, 0])
    total = keep + lax.ppermute(give, "core", SWAP)
    landed = lax.all_to_all(total.astype(jnp.bfloat16), "chip", 0, 0, tiled=True)
    return jnp.sum(landed.astype(jnp.float32), axis=0)


def local(hidden, qkv_weight, out_grad):
    tokens = hidden.shape[0]
    columns = qkv_weight.shape[1]
    total_tokens = tokens * lax.axis_size("chip") * CORES
    scale = float(HD * total_tokens) ** (-0.5)
    grad_scale = float(total_tokens) ** (-0.5)
    proj = jnp.dot(hidden, gathered_weight(qkv_weight), preferred_element_type=jnp.float32)
    count = tokens // BLOCK
    blocks = proj.reshape(count, BLOCK, 3, HD)
    query, keys, values = blocks[:, :, 0], blocks[:, :, 1], blocks[:, :, 2]
    cotangent = out_grad.reshape(count, BLOCK, HD)
    kv_block = jnp.einsum("nsd,nse->nde", keys, values, precision=HIGH)
    qg_block = jnp.einsum("ntd,nte->nde", query, cotangent, precision=HIGH)
    kv_total = jnp.sum(kv_block, axis=0)
    qg_total = jnp.sum(qg_block, axis=0)
    before, after = exchanged_states(kv_total, qg_total)
    prefix = before[None] + jnp.cumsum(kv_block, axis=0) - kv_block
    suffix = after[None] + qg_total[None] - jnp.cumsum(qg_block, axis=0)
    rows = jnp.arange(BLOCK)
    mask = (rows[:, None] >= rows[None, :]).astype(jnp.float32)
    scores = jnp.einsum("ntd,nsd->nts", query, keys, precision=HIGH) * mask
    inner = jnp.einsum("nts,nse->nte", scores, values, precision=HIGH)
    carried = jnp.einsum("ntd,nde->nte", query, prefix, precision=HIGH)
    attended = (scale * (inner + carried)).reshape(tokens, HD)
    dmat = jnp.einsum("nte,nse->nts", cotangent, values, precision=HIGH) * mask
    dquery = scale * (
        jnp.einsum("nts,nsd->ntd", dmat, keys, precision=HIGH)
        + jnp.einsum("nte,nde->ntd", cotangent, prefix, precision=HIGH)
    )
    dkeys = scale * (
        jnp.einsum("nts,ntd->nsd", dmat, query, precision=HIGH)
        + jnp.einsum("nse,nde->nsd", values, suffix, precision=HIGH)
    )
    dvalues = scale * (
        jnp.einsum("nts,nte->nse", scores, cotangent, precision=HIGH)
        + jnp.einsum("nsd,nde->nse", keys, suffix, precision=HIGH)
    )
    dproj = jnp.concatenate([dquery, dkeys, dvalues], axis=2).reshape(tokens, columns)
    product = lax.dot_general(
        hidden,
        dproj.astype(jnp.bfloat16),
        (((0,), (0,)), ((), ())),
        preferred_element_type=jnp.float32,
    )
    return attended, summed_gradient(product) * grad_scale


def solution(mesh):
    chips, heads = mesh.shape["ctx"] // CORES, mesh.shape["head"]
    fine = Mesh(mesh.devices.reshape(chips, CORES, heads), ("chip", "core", "head"))
    return jax.shard_map(
        local,
        mesh=fine,
        in_specs=(P(CTX, None), P(CTX, "head"), P(CTX, "head")),
        out_specs=(P(CTX, "head"), P(CTX, "head")),
        check_vma=False,
    )
```

```python
import functools

import jax
import jax.numpy as jnp
from jax import lax
from jax.experimental import pallas as pl
from jax.experimental.pallas import tpu as pltpu
from jax.sharding import Mesh, PartitionSpec as P

HD = 128
BLOCK = 256
CORES = 2
MIB = 1 << 20

SWAP = [(0, 1), (1, 0)]
CTX = ("chip", "core")
F32 = jnp.float32
BF16 = jnp.bfloat16

PLAIN = (((1,), (0,)), ((), ()))
ROWS = (((1,), (1,)), ((), ()))
COLS = (((0,), (0,)), ((), ()))


def mxu(a, b, dims=PLAIN):
    return lax.dot_general(a, b, dims, preferred_element_type=F32)


def split(x):
    high = x.astype(BF16)
    return high, (x - high.astype(F32)).astype(BF16)


def mxu3(a, b, dims=PLAIN):
    return mxu(a[0], b[0], dims) + (mxu(a[0], b[1], dims) + mxu(a[1], b[0], dims))


def call(body, outs, args, flops, vmem, scratch=(), scalars=0):
    specs = [pl.BlockSpec(memory_space=pltpu.SMEM)] * scalars + [
        pl.BlockSpec(memory_space=pltpu.VMEM)
    ] * (len(args) - scalars)
    size = sum(a.size * a.dtype.itemsize for a in (*args, *outs))
    return pl.pallas_call(
        body,
        out_shape=list(outs),
        in_specs=specs,
        out_specs=[pl.BlockSpec(memory_space=pltpu.VMEM)] * len(outs),
        scratch_shapes=list(scratch),
        cost_estimate=pl.CostEstimate(flops=flops, bytes_accessed=size, transcendentals=0),
        compiler_params=pltpu.CompilerParams(vmem_limit_bytes=vmem * MIB),
    )(*args)


def turn_kernel(core, hidden, keep, give):
    first = core[0] == 0
    group = keep.shape[1]
    for column in range(hidden.shape[1] // HD):
        turned = hidden[:, column * HD : (column + 1) * HD].T
        for pair in range(HD // (CORES * group)):
            at = pair * CORES * group
            even = turned[at : at + group]
            odd = turned[at + group : at + CORES * group]
            chip = column * (HD // (CORES * group)) + pair
            keep[chip] = jnp.where(first, even, odd)
            give[chip] = jnp.where(first, odd, even)


def project_kernel(core, hidden, mine, other, cotangent, proj, parts, weight):
    place = core[0]
    chips, group, columns = mine.shape
    for chip in range(chips):
        weight[2 * chip + place] = mine[chip]
        weight[2 * chip + 1 - place] = other[chip]
    whole = weight[...].reshape(chips * CORES * group, columns)
    kv = jnp.zeros((HD, HD), F32)
    qg = jnp.zeros((HD, HD), F32)
    for start in range(0, hidden.shape[0], BLOCK):
        rows = slice(start, start + BLOCK)
        part = mxu(hidden[rows, :], whole)
        proj[rows, :] = part
        query, keys, values = (split(part[:, j * HD : (j + 1) * HD]) for j in range(3))
        kv += mxu3(keys, values, COLS)
        qg += mxu3(query, split(cotangent[rows, :]), COLS)
    piece = HD // chips
    for chip in range(chips):
        parts[2 * chip] = kv[chip * piece : (chip + 1) * piece]
        parts[2 * chip + 1] = qg[chip * piece : (chip + 1) * piece]


def causal():
    at = lax.broadcasted_iota(jnp.int32, (BLOCK, BLOCK), 0)
    return at >= lax.broadcasted_iota(jnp.int32, (BLOCK, BLOCK), 1)


def local_kernel(proj, cotangent, dlocal):
    tokens = proj.shape[0]
    mask = causal()
    state = jnp.zeros((HD, HD), F32)
    for start in range(0, tokens, BLOCK):
        rows = slice(start, start + BLOCK)
        query, keys, values = (split(proj[rows, j * HD : (j + 1) * HD]) for j in range(3))
        cot = split(cotangent[rows, :])
        scores = split(jnp.where(mask, mxu3(query, keys, ROWS), 0.0))
        dmat = split(jnp.where(mask, mxu3(cot, values, ROWS), 0.0))
        dquery = mxu3(dmat, keys)
        if start:
            dquery += mxu3(cot, split(state), ROWS)
        dlocal[rows, 0:HD] = dquery
        dlocal[rows, HD : 2 * HD] = mxu3(dmat, query, COLS)
        dlocal[rows, 2 * HD : 3 * HD] = mxu3(scores, cot, COLS)
        if start + BLOCK < tokens:
            state += mxu3(keys, values, COLS)
    state = jnp.zeros((HD, HD), F32)
    for start in range(tokens - 2 * BLOCK, -1, -BLOCK):
        later = slice(start + BLOCK, start + 2 * BLOCK)
        rows = slice(start, start + BLOCK)
        state += mxu3(split(proj[later, 0:HD]), split(cotangent[later, :]), COLS)
        suffix = split(state)
        keys, values = split(proj[rows, HD : 2 * HD]), split(proj[rows, 2 * HD : 3 * HD])
        dlocal[rows, HD : 2 * HD] += mxu3(values, suffix, ROWS)
        dlocal[rows, 2 * HD : 3 * HD] += mxu3(keys, suffix)


def scan_kernel(core, pieces, sums):
    devices = pieces.shape[0]
    flip = core[0] == 1
    total = jnp.zeros(pieces.shape[1:], F32)
    for step in range(devices):
        source = jnp.where(flip, devices - 1 - step, step)
        sums[source] = total
        total += pieces[source]


def joined(back, states, which):
    chips, piece = back.shape[0] // CORES, back.shape[1]
    for chip in range(chips):
        states[which, chip * piece : (chip + 1) * piece, :] = back[CORES * chip + which]


def dproj_kernel(scale, back, proj, cotangent, dlocal, dproj, states):
    joined(back, states, 0)
    joined(back, states, 1)
    prefix, suffix = split(states[0]), split(states[1])
    for start in range(0, proj.shape[0], BLOCK):
        rows = slice(start, start + BLOCK)
        keys, values = split(proj[rows, HD : 2 * HD]), split(proj[rows, 2 * HD : 3 * HD])
        cot = split(cotangent[rows, :])
        for j, term in enumerate(
            (
                mxu3(cot, prefix, ROWS),
                mxu3(values, suffix, ROWS),
                mxu3(keys, suffix),
            )
        ):
            columns = slice(j * HD, (j + 1) * HD)
            dproj[rows, columns] = (scale * (dlocal[rows, columns] + term)).astype(BF16)


def attended_kernel(scale, back, proj, attended, states):
    joined(back, states, 0)
    state = states[0]
    mask = causal()
    for start in range(0, proj.shape[0], BLOCK):
        rows = slice(start, start + BLOCK)
        query, keys, values = (split(proj[rows, j * HD : (j + 1) * HD]) for j in range(3))
        scores = split(jnp.where(mask, mxu3(query, keys, ROWS), 0.0))
        attended[rows, :] = scale * (mxu3(scores, values) + mxu3(query, split(state)))
        state += mxu3(keys, values, COLS)


def own_kernel(turned, dproj, product):
    for start in range(0, turned.shape[0], BLOCK):
        rows = slice(start, start + BLOCK)
        product[rows, :] = mxu(turned[rows, :], dproj[...])


def total_kernel(turned, dproj, product, total):
    for start in range(0, turned.shape[0], BLOCK):
        rows = slice(start, start + BLOCK)
        total[rows, :] = (product[rows, :] + mxu(turned[rows, :], dproj[...])).astype(BF16)


def shape(dims, dtype=F32):
    return jax.ShapeDtypeStruct(dims, dtype)


def local(hidden, qkv_weight, out_grad):
    tokens, width = hidden.shape
    group, columns = qkv_weight.shape
    chips = lax.axis_size("chip")
    devices = chips * CORES
    piece = HD // chips
    total_tokens = tokens * devices
    scale = float(HD * total_tokens) ** (-0.5)
    grad_scale = float(total_tokens) ** (-0.5)
    core = lax.axis_index("core").astype(jnp.int32).reshape(1)
    half = width // CORES

    spread = jnp.broadcast_to(qkv_weight[None], (chips, group, columns))
    mine = lax.all_to_all(spread, "chip", 0, 0, tiled=True)
    keep, give = call(
        turn_kernel,
        [shape((chips, group, tokens), BF16)] * 2,
        [core, hidden],
        tokens * width * 1024,
        24,
        scalars=1,
    )
    mine, keep, give = lax.optimization_barrier((mine, keep, give))
    keep, give = keep.reshape(half, tokens), give.reshape(half, tokens)
    taken = lax.ppermute(give, "core", SWAP)
    other = lax.ppermute(mine, "core", SWAP)

    proj, parts = call(
        project_kernel,
        [shape((tokens, columns)), shape((devices, piece, HD))],
        [core, hidden, mine, other, out_grad],
        2 * tokens * width * columns + 12 * tokens * HD * HD,
        32,
        [pltpu.VMEM((devices, group, columns), BF16)],
        scalars=1,
    )
    pieces = lax.all_to_all(parts, CTX, 0, 0, tiled=True)
    (dlocal,) = call(
        local_kernel,
        [shape((tokens, columns))],
        [proj, out_grad],
        15 * 6 * tokens * HD * HD,
        24,
    )
    pieces, dlocal = lax.optimization_barrier((pieces, dlocal))
    (sums,) = call(
        scan_kernel, [shape(parts.shape)], [core, pieces], devices * HD * HD, 8, scalars=1
    )
    back = lax.all_to_all(sums, CTX, 0, 0, tiled=True)

    states = [pltpu.VMEM((2, HD, HD), F32)]
    (dproj,) = call(
        functools.partial(dproj_kernel, scale),
        [shape((tokens, columns), BF16)],
        [back, proj, out_grad, dlocal],
        18 * tokens * HD * HD,
        24,
        states,
    )
    theirs = lax.ppermute(dproj, "core", SWAP)
    (product,) = call(
        own_kernel,
        [shape((half, columns))],
        [keep, dproj],
        2 * half * tokens * columns,
        24,
    )
    (total,) = call(
        total_kernel,
        [shape((half, columns), BF16)],
        [taken, theirs, product],
        2 * half * tokens * columns,
        24,
    )
    landed = lax.all_to_all(total.reshape(chips, group, columns), "chip", 0, 0, tiled=True)
    (attended,) = call(
        functools.partial(attended_kernel, scale),
        [shape((tokens, HD))],
        [back, proj],
        6 * 6 * tokens * HD * HD,
        24,
        states,
    )
    return attended, jnp.sum(landed.astype(F32), axis=0) * grad_scale


def solution(mesh):
    chips, heads = mesh.shape["ctx"] // CORES, mesh.shape["head"]
    fine = Mesh(mesh.devices.reshape(chips, CORES, heads), ("chip", "core", "head"))
    return jax.shard_map(
        local,
        mesh=fine,
        in_specs=(P(CTX, None), P(CTX, "head"), P(CTX, "head")),
        out_specs=(P(CTX, "head"), P(CTX, "head")),
        check_vma=False,
    )
```

```python
import functools

import jax
import jax.numpy as jnp
from jax import lax
from jax.experimental import pallas as pl
from jax.experimental.pallas import tpu as pltpu
from jax.sharding import Mesh, PartitionSpec as P

HD = 128
BLOCK = 256
CORES = 2
MIB = 1 << 20

SWAP = [(0, 1), (1, 0)]
CTX = ("chip", "core")
F32 = jnp.float32
BF16 = jnp.bfloat16

PLAIN = (((1,), (0,)), ((), ()))
ROWS = (((1,), (1,)), ((), ()))
COLS = (((0,), (0,)), ((), ()))


def mxu(a, b, dims=PLAIN):
    return lax.dot_general(a, b, dims, preferred_element_type=F32)


def split(x):
    high = x.astype(BF16)
    return high, (x - high.astype(F32)).astype(BF16)


def mxu3(a, b, dims=PLAIN):
    return mxu(a[0], b[0], dims) + (mxu(a[0], b[1], dims) + mxu(a[1], b[0], dims))


HBM = pl.BlockSpec(memory_space=pltpu.HBM)
VMEM = pl.BlockSpec(memory_space=pltpu.VMEM)
SMEM = pl.BlockSpec(memory_space=pltpu.SMEM)


def call(body, outs, args, flops, vmem, specs, scratch=(), kind=jax.ShapeDtypeStruct):
    size = sum(a.size * a.dtype.itemsize for a in args)
    args = [
        pltpu.with_memory_space_constraint(a, pltpu.HBM) if spec is HBM else a
        for a, spec in zip(args, specs)
    ]
    return pl.pallas_call(
        body,
        out_shape=[kind(dims, dtype) for dims, dtype in outs],
        in_specs=specs,
        out_specs=[VMEM] * len(outs),
        scratch_shapes=list(scratch),
        cost_estimate=pl.CostEstimate(flops=flops, bytes_accessed=size, transcendentals=0),
        compiler_params=pltpu.CompilerParams(vmem_limit_bytes=vmem * MIB),
    )(*args)


def causal():
    at = lax.broadcasted_iota(jnp.int32, (BLOCK, BLOCK), 0)
    return at >= lax.broadcasted_iota(jnp.int32, (BLOCK, BLOCK), 1)


def blocks(tokens):
    return [
        (slab, slice(start, start + BLOCK))
        for slab in range(CORES)
        for start in range(0, tokens, BLOCK)
    ]


def pieces_of(ref, slab, rows):
    return tuple(split(ref[slab, rows, j * HD : (j + 1) * HD]) for j in range(3))


def spread_kernel(weight, copies):
    for chip in range(copies.shape[0]):
        copies[chip] = weight[...]


def prepare_kernel(group, core, hidden, partner, cot, cot_partner, near, far, turned, cots):
    cots[core[0]] = cot[...]
    cots[1 - core[0]] = cot_partner[...]
    wide = 2 * HD
    at = lax.broadcasted_iota(jnp.int32, (wide, wide), 0)
    to = lax.broadcasted_iota(jnp.int32, (wide, wide), 1)
    parity = jnp.where(to < HD, core[0], 1 - core[0])
    slot = lax.rem(to, HD)
    source = (lax.div(slot, group) * CORES + parity) * group + lax.rem(slot, group)
    order = jnp.where(at == source, 1.0, 0.0).astype(BF16)
    for which, rows in ((core[0], hidden), (1 - core[0], partner)):
        for step in range(hidden.shape[1] // wide):
            columns = mxu(rows[:, step * wide : (step + 1) * wide], order).astype(BF16)
            span = slice(step * HD, (step + 1) * HD)
            near[which, :, span] = columns[:, :HD]
            far[which, :, span] = columns[:, HD:]
            turned[which, span, :] = columns[:, :HD].T


def half_kernel(near, mine, partial):
    chips, group, columns = mine.shape
    weight = mine[...].reshape(chips * group, columns)
    for slab, rows in blocks(near.shape[1]):
        partial[slab, rows, :] = mxu(near[slab, rows, :], weight)


def project_kernel(core, far, theirs, partial, cots, proj, parts):
    chips, group, columns = theirs.shape
    weight = theirs[...].reshape(chips * group, columns)
    first = core[0] == 0
    state = jnp.zeros((HD, HD), F32)
    for slab, rows in blocks(far.shape[1]):
        part = partial[slab, rows, :] + mxu(far[slab, rows, :], weight)
        proj[slab, rows, :] = part
        cotangent = cots[slab, rows, :]
        left = jnp.where(first, part[:, HD : 2 * HD], part[:, :HD])
        right = jnp.where(first, part[:, 2 * HD :], cotangent)
        state += mxu3(split(left), split(right), COLS)
    piece = HD // chips
    for chip in range(chips):
        parts[chip] = state[chip * piece : (chip + 1) * piece]


def local_kernel(proj, cots, dlocal, states):
    mask = causal()
    state = jnp.zeros((HD, HD), F32)
    for slab, rows in blocks(proj.shape[1]):
        if slab and rows.start == 0:
            states[...] = state
        query, keys, values = pieces_of(proj, slab, rows)
        cot = split(cots[slab, rows, :])
        scores = split(jnp.where(mask, mxu3(query, keys, ROWS), 0.0))
        dmat = split(jnp.where(mask, mxu3(cot, values, ROWS), 0.0))
        dlocal[slab, rows, 0:HD] = mxu3(dmat, keys) + mxu3(cot, split(state), ROWS)
        dlocal[slab, rows, HD : 2 * HD] = mxu3(dmat, query, COLS)
        dlocal[slab, rows, 2 * HD :] = mxu3(scores, cot, COLS)
        state += mxu3(keys, values, COLS)


def later_kernel(proj, cots, dlocal, out):
    state = jnp.zeros((HD, HD), F32)
    for slab, rows in reversed(blocks(proj.shape[1])):
        query, keys, values = pieces_of(proj, slab, rows)
        suffix = split(state)
        out[slab, rows, 0:HD] = dlocal[slab, rows, 0:HD]
        out[slab, rows, HD : 2 * HD] = dlocal[slab, rows, HD : 2 * HD] + mxu3(
            values, suffix, ROWS
        )
        out[slab, rows, 2 * HD :] = dlocal[slab, rows, 2 * HD :] + mxu3(keys, suffix)
        state += mxu3(query, split(cots[slab, rows, :]), COLS)


def scan_kernel(core, pieces, sums):
    chips = pieces.shape[0]
    flip = core[0] == 1
    total = jnp.zeros(pieces.shape[1:], F32)
    for step in range(chips):
        chip = jnp.where(flip, chips - 1 - step, step)
        for member in range(CORES):
            sums[CORES * chip + member] = total
        total += pieces[chip]


def joined(back, which, states):
    chips, piece = back.shape[0] // CORES, back.shape[1]
    for chip in range(chips):
        states[which, chip * piece : (chip + 1) * piece, :] = back[CORES * chip + which]
    return states[which]


def finish_kernel(scale, back, proj, cots, dlocal, turned, total,
                  kv, cot, part, rows_turned, dproj, states, sems):
    tokens = cots.shape[1]
    loads = []
    for index, (slab, rows) in enumerate(blocks(tokens)):
        loads.append(
            [
                pltpu.make_async_copy(source, target, sems.at[index, which])
                for which, (source, target) in enumerate(
                    (
                        (proj.at[slab, rows, pl.ds(HD, 2 * HD)], kv.at[slab, rows, :]),
                        (cots.at[slab, rows, :], cot.at[slab, rows, :]),
                        (dlocal.at[slab, rows, :], part.at[slab, rows, :]),
                    )
                )
            ]
        )
    last = len(loads)
    loads.append(
        [
            pltpu.make_async_copy(turned.at[slab], rows_turned.at[slab], sems.at[last, slab])
            for slab in range(CORES)
        ]
    )
    for group in loads:
        for load in group:
            load.start()
    before, after = joined(back, 0, states), joined(back, 1, states)
    prefix, suffix, suffix_turned = split(before.T), split(after), split(after.T)
    for index, (slab, rows) in enumerate(blocks(tokens)):
        for load in loads[index]:
            load.wait()
        keys, values = split(kv[slab, rows, :HD]), split(kv[slab, rows, HD:])
        for j, term in enumerate(
            (
                mxu3(split(cot[slab, rows, :]), prefix),
                mxu3(values, suffix_turned),
                mxu3(keys, suffix),
            )
        ):
            columns = slice(j * HD, (j + 1) * HD)
            dproj[slab, rows, columns] = (scale * (part[slab, rows, columns] + term)).astype(BF16)
    for load in loads[last]:
        load.wait()
    for start in range(0, turned.shape[1], BLOCK):
        rows = slice(start, start + BLOCK)
        total[rows, :] = (
            mxu(rows_turned[0, rows, :], dproj[0]) + mxu(rows_turned[1, rows, :], dproj[1])
        ).astype(BF16)


def attended_kernel(scale, core, back, early, proj, attended, states):
    tokens = proj.shape[1]
    before = joined(back, 0, states)
    state = jnp.where(core[0] == 0, before, before + early[...])
    mask = causal()
    for start in range(0, tokens, BLOCK):
        rows = slice(start, start + BLOCK)
        query, keys, values = pieces_of(proj, core[0], rows)
        scores = split(jnp.where(mask, mxu3(query, keys, ROWS), 0.0))
        attended[rows, :] = scale * (mxu3(scores, values) + mxu3(query, split(state)))
        state += mxu3(keys, values, COLS)


def local(hidden, qkv_weight, out_grad):
    tokens, width = hidden.shape
    group, columns = qkv_weight.shape
    chips = lax.axis_size("chip")
    devices = chips * CORES
    piece = HD // chips
    half = width // CORES
    total_tokens = tokens * devices
    scale = float(HD * total_tokens) ** (-0.5)
    grad_scale = float(total_tokens) ** (-0.5)
    core = lax.axis_index("core").astype(jnp.int32).reshape(1)
    square = CORES * tokens * HD * HD
    product = 2 * CORES * tokens * half * columns

    (copies,) = call(spread_kernel, [((chips, group, columns), BF16)], [qkv_weight], 1024, 8, [VMEM])
    mine = lax.all_to_all(copies, "chip", 0, 0, tiled=True)
    partner = lax.ppermute(hidden, "core", SWAP)
    cot_partner = lax.ppermute(out_grad, "core", SWAP)
    near, far, turned, cots = call(
        functools.partial(prepare_kernel, group),
        [((CORES, tokens, half), BF16)] * 2 + [
            ((CORES, half, tokens), BF16),
            ((CORES, tokens, HD), F32),
        ],
        [core, hidden, partner, out_grad, cot_partner],
        2 * tokens * width * 1024,
        40,
        [SMEM] + [VMEM] * 4,
    )
    mine, near, far, turned, cots = lax.optimization_barrier((mine, near, far, turned, cots))
    theirs = lax.ppermute(mine, "core", SWAP)
    (partial,) = call(
        half_kernel, [((CORES, tokens, columns), F32)], [near, mine], product, 24, [VMEM, VMEM]
    )
    proj, parts = call(
        project_kernel,
        [((CORES, tokens, columns), F32), ((chips, piece, HD), F32)],
        [core, far, theirs, partial, cots],
        product + 6 * square,
        32,
        [SMEM] + [VMEM] * 4,
    )
    pieces = lax.all_to_all(parts, "chip", 0, 0, tiled=True)
    dlocal, early = call(
        local_kernel,
        [((CORES, tokens, columns), F32), ((HD, HD), F32)],
        [proj, cots],
        12 * 6 * square,
        32,
        [VMEM, VMEM],
    )
    pieces, dlocal = lax.optimization_barrier((pieces, dlocal))
    (sums,) = call(
        scan_kernel, [((devices, piece, HD), F32)], [core, pieces], 4 * HD * HD, 8, [SMEM, VMEM]
    )
    back = lax.all_to_all(sums, CTX, 0, 0, tiled=True)
    (dlocal,) = call(
        later_kernel,
        [((CORES, tokens, columns), F32)],
        [proj, cots, dlocal],
        3 * 6 * square,
        32,
        [VMEM] * 3,
    )
    (total,) = call(
        functools.partial(finish_kernel, scale),
        [((half, columns), BF16)],
        [back, proj, cots, dlocal, turned],
        18 * square + product,
        32,
        [VMEM] + [HBM] * 4,
        [
            pltpu.VMEM((CORES, tokens, 2 * HD), F32),
            pltpu.VMEM((CORES, tokens, HD), F32),
            pltpu.VMEM((CORES, tokens, columns), F32),
            pltpu.VMEM((CORES, half, tokens), BF16),
            pltpu.VMEM((CORES, tokens, columns), BF16),
            pltpu.VMEM((2, HD, HD), F32),
            pltpu.SemaphoreType.DMA((CORES * tokens // BLOCK + 1, 3)),
        ],
        pltpu.HBM,
    )
    landed = lax.all_to_all(total.reshape(chips, group, columns), "chip", 0, 0, tiled=True)
    (attended,) = call(
        functools.partial(attended_kernel, scale),
        [((tokens, HD), F32)],
        [core, back, early, proj],
        6 * 6 * square,
        24,
        [SMEM] + [VMEM] * 3,
        [pltpu.VMEM((2, HD, HD), F32)],
    )
    return attended, jnp.sum(landed.astype(F32), axis=0) * grad_scale


def solution(mesh):
    chips, heads = mesh.shape["ctx"] // CORES, mesh.shape["head"]
    fine = Mesh(mesh.devices.reshape(chips, CORES, heads), ("chip", "core", "head"))
    return jax.shard_map(
        local,
        mesh=fine,
        in_specs=(P(CTX, None), P(CTX, "head"), P(CTX, "head")),
        out_specs=(P(CTX, "head"), P(CTX, "head")),
        check_vma=False,
    )
```

```python
import functools

import jax
import jax.numpy as jnp
from jax import lax
from jax.experimental import pallas as pl
from jax.experimental.pallas import tpu as pltpu
from jax.sharding import Mesh, PartitionSpec as P

HD = 128
BLOCK = 256
CORES = 2
MIB = 1 << 20

SWAP = [(0, 1), (1, 0)]
CTX = ("chip", "core")
F32 = jnp.float32
BF16 = jnp.bfloat16

PLAIN = (((1,), (0,)), ((), ()))
ROWS = (((1,), (1,)), ((), ()))
COLS = (((0,), (0,)), ((), ()))


def mxu(a, b, dims=PLAIN):
    return lax.dot_general(a, b, dims, preferred_element_type=F32)


def split(x):
    high = x.astype(BF16)
    return high, (x - high.astype(F32)).astype(BF16)


def beside(x):
    return jnp.concatenate(split(x), axis=1)


def doubled(x):
    both = beside(x)
    return jnp.concatenate([both, both], axis=0)


def folded(out):
    width = out.shape[1] // 2
    return out[:, :width] + out[:, width:]


def times(left, right):
    return folded(mxu(left, right))


def gram(left, right):
    out = folded(mxu(left, right, COLS))
    height = out.shape[0] // 2
    return out[:height] + out[height:]


def cross(left, right):
    high, low = split(right)
    return mxu(left, jnp.concatenate([high, high], axis=1), ROWS) + mxu(
        left, jnp.concatenate([low, low], axis=1), ROWS
    )


HBM = pl.BlockSpec(memory_space=pltpu.HBM)
VMEM = pl.BlockSpec(memory_space=pltpu.VMEM)
SMEM = pl.BlockSpec(memory_space=pltpu.SMEM)


def vmem(dims, dtype=F32):
    return jax.ShapeDtypeStruct(dims, dtype), VMEM


def hbm(dims, dtype=F32):
    return pltpu.HBM(dims, dtype), VMEM


def direct(dims, dtype=F32):
    return pltpu.HBM(dims, dtype), HBM


def call(body, outs, args, flops, limit, specs, scratch=()):
    size = sum(a.size * a.dtype.itemsize for a in args)
    args = [
        pltpu.with_memory_space_constraint(a, pltpu.HBM) if spec is HBM else a
        for a, spec in zip(args, specs)
    ]
    return pl.pallas_call(
        body,
        out_shape=[kind for kind, _ in outs],
        in_specs=specs,
        out_specs=[spec for _, spec in outs],
        scratch_shapes=list(scratch),
        cost_estimate=pl.CostEstimate(flops=flops, bytes_accessed=size, transcendentals=0),
        compiler_params=pltpu.CompilerParams(vmem_limit_bytes=limit * MIB),
    )(*args)


def chunks(total):
    return [slice(start, start + BLOCK) for start in range(0, total, BLOCK)]


def fetched(source, target, sems):
    loads = [
        pltpu.make_async_copy(source.at[rows, :], target.at[rows, :], sems.at[index])
        for index, rows in enumerate(chunks(source.shape[0]))
    ]
    for load in loads:
        load.start()
    return loads


def causal():
    at = lax.broadcasted_iota(jnp.int32, (BLOCK, BLOCK), 0)
    return at >= lax.broadcasted_iota(jnp.int32, (BLOCK, BLOCK), 1)


def spread_kernel(weight, copies, sems):
    copying = [
        pltpu.make_async_copy(weight, copies.at[chip], sems.at[chip])
        for chip in range(copies.shape[0])
    ]
    for each in copying:
        each.start()
    for each in copying:
        each.wait()


def turn_kernel(core, hidden, keep, give):
    first = core[0] == 0
    group = keep.shape[1]
    for column in range(hidden.shape[1] // HD):
        turned = hidden[:, column * HD : (column + 1) * HD].T
        for pair in range(HD // (CORES * group)):
            at = pair * CORES * group
            even = turned[at : at + group]
            odd = turned[at + group : at + CORES * group]
            chip = column * (HD // (CORES * group)) + pair
            keep[chip] = jnp.where(first, even, odd)
            give[chip] = jnp.where(first, odd, even)


def project_kernel(core, hidden, mine, other, cotangent, query, kv, parts, rows_in, weight, sems):
    loads = fetched(hidden, rows_in, sems)
    place = core[0]
    chips, group, columns = mine.shape
    for chip in range(chips):
        weight[2 * chip + place] = mine[chip]
        weight[2 * chip + 1 - place] = other[chip]
    whole = weight[...].reshape(chips * CORES * group, columns)
    kv_state = jnp.zeros((HD, HD), F32)
    qg_state = jnp.zeros((HD, HD), F32)
    for load, rows in zip(loads, chunks(hidden.shape[0])):
        load.wait()
        part = mxu(rows_in[rows, :], whole)
        query[rows, :] = part[:, :HD]
        kv[rows, :] = part[:, HD:]
        kv_state += gram(beside(part[:, HD : 2 * HD]), beside(part[:, 2 * HD :]))
        qg_state += gram(beside(part[:, :HD]), beside(cotangent[rows, :]))
    piece = HD // chips
    for chip in range(chips):
        parts[2 * chip] = kv_state[chip * piece : (chip + 1) * piece]
        parts[2 * chip + 1] = qg_state[chip * piece : (chip + 1) * piece]


def local_kernel(query, kv, cotangent, dlocal):
    mask = causal()
    order = chunks(query.shape[0])
    state = jnp.zeros((HD, HD), F32)
    for rows in order:
        keys, values = kv[rows, :HD], kv[rows, HD:]
        queries, cot = beside(query[rows, :]), beside(cotangent[rows, :])
        scores = jnp.where(mask, cross(queries, keys), 0.0)
        dmat = jnp.where(mask, cross(cot, values), 0.0)
        dquery = times(beside(dmat), doubled(keys))
        if rows is not order[0]:
            dquery += times(cot, doubled(state.T))
        dlocal[rows, 0:HD] = dquery
        dlocal[rows, HD : 2 * HD] = gram(beside(dmat), queries)
        dlocal[rows, 2 * HD :] = gram(beside(scores), cot)
        if rows is not order[-1]:
            state += gram(beside(keys), beside(values))
    state = jnp.zeros((HD, HD), F32)
    for later, rows in zip(order[:0:-1], order[-2::-1]):
        state += gram(beside(query[later, :]), beside(cotangent[later, :]))
        dlocal[rows, HD : 2 * HD] += times(beside(kv[rows, HD:]), doubled(state.T))
        dlocal[rows, 2 * HD :] += times(beside(kv[rows, :HD]), doubled(state))


def scan_kernel(core, pieces, sums):
    devices = pieces.shape[0]
    flip = core[0] == 1
    total = jnp.zeros(pieces.shape[1:], F32)
    for step in range(devices):
        source = jnp.where(flip, devices - 1 - step, step)
        sums[source] = total
        total += pieces[source]


def joined(back, which, states):
    chips, piece = back.shape[0] // CORES, back.shape[1]
    for chip in range(chips):
        states[which, chip * piece : (chip + 1) * piece, :] = back[CORES * chip + which]
    return states[which]


def dproj_kernel(scale, back, kv, cotangent, dlocal, dproj, states):
    before, after = joined(back, 0, states), joined(back, 1, states)
    prefix, suffix, turned = doubled(before.T), doubled(after), doubled(after.T)
    for rows in chunks(kv.shape[0]):
        for j, term in enumerate(
            (
                times(beside(cotangent[rows, :]), prefix),
                times(beside(kv[rows, HD:]), turned),
                times(beside(kv[rows, :HD]), suffix),
            )
        ):
            columns = slice(j * HD, (j + 1) * HD)
            dproj[rows, columns] = (scale * (dlocal[rows, columns] + term)).astype(BF16)


def attended_kernel(scale, back, query, kv, attended, states):
    state = joined(back, 0, states)
    mask = causal()
    for rows in chunks(query.shape[0]):
        keys, values = kv[rows, :HD], kv[rows, HD:]
        queries = beside(query[rows, :])
        scores = jnp.where(mask, cross(queries, keys), 0.0)
        attended[rows, :] = scale * (
            times(beside(scores), doubled(values)) + times(queries, doubled(state))
        )
        state += gram(beside(keys), beside(values))


def own_kernel(turned, dproj, product):
    for rows in chunks(turned.shape[0]):
        product[rows, :] = mxu(turned[rows, :], dproj[...])


def total_kernel(turned, dproj, product, total, rows_in, sems):
    loads = fetched(turned, rows_in, sems)
    for load, rows in zip(loads, chunks(turned.shape[0])):
        load.wait()
        total[rows, :] = (product[rows, :] + mxu(rows_in[rows, :], dproj[...])).astype(BF16)


def sum_kernel(scale, landed, grad):
    total = landed[0].astype(F32)
    for chip in range(1, landed.shape[0]):
        total += landed[chip].astype(F32)
    grad[...] = scale * total


def local(hidden, qkv_weight, out_grad):
    tokens, width = hidden.shape
    group, columns = qkv_weight.shape
    chips = lax.axis_size("chip")
    devices = chips * CORES
    piece = HD // chips
    total_tokens = tokens * devices
    scale = float(HD * total_tokens) ** (-0.5)
    grad_scale = float(total_tokens) ** (-0.5)
    core = lax.axis_index("core").astype(jnp.int32).reshape(1)
    half = width // CORES
    square = tokens * HD * HD
    states = [pltpu.VMEM((2, HD, HD), F32)]

    (copies,) = call(
        spread_kernel,
        [direct((chips, group, columns), BF16)],
        [qkv_weight],
        1024,
        8,
        [HBM],
        [pltpu.SemaphoreType.DMA((chips,))],
    )
    mine = lax.all_to_all(copies, "chip", 0, 0, tiled=True)
    keep, give = call(
        turn_kernel,
        [hbm((chips, group, tokens), BF16)] * 2,
        [core, hidden],
        tokens * width * 1024,
        24,
        [SMEM, VMEM],
    )
    mine, keep, give = lax.optimization_barrier((mine, keep, give))
    keep, give = keep.reshape(half, tokens), give.reshape(half, tokens)
    taken = lax.ppermute(give, "core", SWAP)
    other = lax.ppermute(mine, "core", SWAP)

    query, kv, parts = call(
        project_kernel,
        [hbm((tokens, HD)), vmem((tokens, 2 * HD)), vmem((devices, piece, HD))],
        [core, hidden, mine, other, out_grad],
        2 * tokens * width * columns + 16 * square,
        32,
        [SMEM, HBM, VMEM, VMEM, VMEM],
        [
            pltpu.VMEM((tokens, width), BF16),
            pltpu.VMEM((devices, group, columns), BF16),
            pltpu.SemaphoreType.DMA((tokens // BLOCK,)),
        ],
    )
    pieces = lax.all_to_all(parts, CTX, 0, 0, tiled=True)
    (dlocal,) = call(
        local_kernel,
        [vmem((tokens, columns))],
        [query, kv, out_grad],
        15 * 6 * square,
        24,
        [VMEM] * 3,
    )
    pieces, dlocal = lax.optimization_barrier((pieces, dlocal))
    (sums,) = call(
        scan_kernel, [vmem(parts.shape)], [core, pieces], devices * HD * HD, 8, [SMEM, VMEM]
    )
    back = lax.all_to_all(sums, CTX, 0, 0, tiled=True)

    (dproj,) = call(
        functools.partial(dproj_kernel, scale),
        [vmem((tokens, columns), BF16)],
        [back, kv, out_grad, dlocal],
        24 * square,
        24,
        [VMEM] * 4,
        states,
    )
    theirs = lax.ppermute(dproj, "core", SWAP)
    (product,) = call(
        own_kernel,
        [vmem((half, columns))],
        [keep, dproj],
        2 * half * tokens * columns,
        24,
        [VMEM] * 2,
    )
    (total,) = call(
        total_kernel,
        [hbm((half, columns), BF16)],
        [taken, theirs, product],
        2 * half * tokens * columns,
        24,
        [HBM, VMEM, VMEM],
        [pltpu.VMEM((half, tokens), BF16), pltpu.SemaphoreType.DMA((half // BLOCK,))],
    )
    landed = lax.all_to_all(total.reshape(chips, group, columns), "chip", 0, 0, tiled=True)
    (attended,) = call(
        functools.partial(attended_kernel, scale),
        [hbm((tokens, HD))],
        [back, query, kv],
        6 * 6 * square,
        24,
        [VMEM] * 3,
        states,
    )
    (grad,) = call(
        functools.partial(sum_kernel, grad_scale),
        [hbm((group, columns))],
        [landed],
        half * columns,
        16,
        [VMEM],
    )
    return attended, grad


def solution(mesh):
    chips, heads = mesh.shape["ctx"] // CORES, mesh.shape["head"]
    fine = Mesh(mesh.devices.reshape(chips, CORES, heads), ("chip", "core", "head"))
    return jax.shard_map(
        local,
        mesh=fine,
        in_specs=(P(CTX, None), P(CTX, "head"), P(CTX, "head")),
        out_specs=(P(CTX, "head"), P(CTX, "head")),
        check_vma=False,
    )
```

```python
import functools

import jax
import jax.numpy as jnp
from jax import lax
from jax.experimental import pallas as pl
from jax.experimental.pallas import tpu as pltpu
from jax.sharding import Mesh, PartitionSpec as P

HD = 128
BLOCK = 256
CORES = 2
MIB = 1 << 20

SWAP = [(0, 1), (1, 0)]
CTX = ("chip", "core")
F32 = jnp.float32
BF16 = jnp.bfloat16

PLAIN = (((1,), (0,)), ((), ()))
ROWS = (((1,), (1,)), ((), ()))
COLS = (((0,), (0,)), ((), ()))


def mxu(a, b, dims=PLAIN):
    return lax.dot_general(a, b, dims, preferred_element_type=F32)


def split(x):
    high = x.astype(BF16)
    return high, (x - high.astype(F32)).astype(BF16)


def beside(x):
    return jnp.concatenate(split(x), axis=1)


def doubled(x):
    both = beside(x)
    return jnp.concatenate([both, both], axis=0)


def folded(out):
    width = out.shape[1] // 2
    return out[:, :width] + out[:, width:]


def times(left, right):
    return folded(mxu(left, right))


def gram(left, right):
    out = folded(mxu(left, right, COLS))
    height = out.shape[0] // 2
    return out[:height] + out[height:]


def cross(left, right):
    high, low = split(right)
    return mxu(left, jnp.concatenate([high, high], axis=1), ROWS) + mxu(
        left, jnp.concatenate([low, low], axis=1), ROWS
    )


HBM = pl.BlockSpec(memory_space=pltpu.HBM)
VMEM = pl.BlockSpec(memory_space=pltpu.VMEM)
SMEM = pl.BlockSpec(memory_space=pltpu.SMEM)


def vmem(dims, dtype=F32):
    return jax.ShapeDtypeStruct(dims, dtype), VMEM


def hbm(dims, dtype=F32):
    return pltpu.HBM(dims, dtype), VMEM


def direct(dims, dtype=F32):
    return pltpu.HBM(dims, dtype), HBM


def call(body, outs, args, flops, limit, specs, scratch=()):
    size = sum(a.size * a.dtype.itemsize for a in args)
    args = [
        pltpu.with_memory_space_constraint(a, pltpu.HBM) if spec is HBM else a
        for a, spec in zip(args, specs)
    ]
    return pl.pallas_call(
        body,
        out_shape=[kind for kind, _ in outs],
        in_specs=specs,
        out_specs=[spec for _, spec in outs],
        scratch_shapes=list(scratch),
        cost_estimate=pl.CostEstimate(flops=flops, bytes_accessed=size, transcendentals=0),
        compiler_params=pltpu.CompilerParams(vmem_limit_bytes=limit * MIB),
    )(*args)


def chunks(total):
    return [slice(start, start + BLOCK) for start in range(0, total, BLOCK)]


def fetched(source, target, sems):
    loads = [
        pltpu.make_async_copy(source.at[rows, :], target.at[rows, :], sems.at[index])
        for index, rows in enumerate(chunks(source.shape[0]))
    ]
    for load in loads:
        load.start()
    return loads


def causal():
    at = lax.broadcasted_iota(jnp.int32, (BLOCK, BLOCK), 0)
    return at >= lax.broadcasted_iota(jnp.int32, (BLOCK, BLOCK), 1)


def spread_kernel(weight, copies):
    for chip in range(copies.shape[0]):
        copies[chip] = weight[...]


def turn_kernel(core, hidden, keep, give, head):
    head[...] = hidden[: head.shape[0], :]
    first = core[0] == 0
    group = keep.shape[1]
    for column in range(hidden.shape[1] // HD):
        turned = hidden[:, column * HD : (column + 1) * HD].T
        for pair in range(HD // (CORES * group)):
            at = pair * CORES * group
            even = turned[at : at + group]
            odd = turned[at + group : at + CORES * group]
            chip = column * (HD // (CORES * group)) + pair
            keep[chip] = jnp.where(first, even, odd)
            give[chip] = jnp.where(first, odd, even)


def project_kernel(core, hidden, head, mine, other, cotangent, query, kv, parts,
                   tail, weight, proj, load_sem, sems):
    ahead = head.shape[0]
    load = pltpu.make_async_copy(hidden.at[ahead:, :], tail, load_sem)
    load.start()
    stores = []
    place = core[0]
    chips, group, columns = mine.shape
    for chip in range(chips):
        weight[2 * chip + place] = mine[chip]
        weight[2 * chip + 1 - place] = other[chip]
    whole = weight[...].reshape(chips * CORES * group, columns)
    kv_state = jnp.zeros((HD, HD), F32)
    qg_state = jnp.zeros((HD, HD), F32)
    for base, held in ((0, head), (ahead, tail)):
        if base:
            load.wait()
        for rows in chunks(held.shape[0]):
            part = mxu(held[rows, :], whole)
            to = slice(base + rows.start, base + rows.stop)
            proj[to, :] = part
            for which, target, columns in ((0, query, pl.ds(0, HD)), (1, kv, pl.ds(HD, 2 * HD))):
                stores.append(
                    pltpu.make_async_copy(
                        proj.at[to, columns], target.at[to, :], sems.at[len(stores) // 2, which]
                    )
                )
                stores[-1].start()
            kv_state += gram(beside(part[:, HD : 2 * HD]), beside(part[:, 2 * HD :]))
            qg_state += gram(beside(part[:, :HD]), beside(cotangent[to, :]))
    piece = HD // chips
    for chip in range(chips):
        parts[2 * chip] = kv_state[chip * piece : (chip + 1) * piece]
        parts[2 * chip + 1] = qg_state[chip * piece : (chip + 1) * piece]
    for store in stores:
        store.wait()


def local_kernel(query, kv, cotangent, dlocal):
    mask = causal()
    order = chunks(query.shape[0])
    state = jnp.zeros((HD, HD), F32)
    for rows in order:
        keys, values = kv[rows, :HD], kv[rows, HD:]
        queries, cot = beside(query[rows, :]), beside(cotangent[rows, :])
        scores = jnp.where(mask, cross(queries, keys), 0.0)
        dmat = jnp.where(mask, cross(cot, values), 0.0)
        dquery = times(beside(dmat), doubled(keys))
        if rows is not order[0]:
            dquery += times(cot, doubled(state.T))
        dlocal[rows, 0:HD] = dquery
        dlocal[rows, HD : 2 * HD] = gram(beside(dmat), queries)
        dlocal[rows, 2 * HD :] = gram(beside(scores), cot)
        if rows is not order[-1]:
            state += gram(beside(keys), beside(values))
    state = jnp.zeros((HD, HD), F32)
    for later, rows in zip(order[:0:-1], order[-2::-1]):
        state += gram(beside(query[later, :]), beside(cotangent[later, :]))
        dlocal[rows, HD : 2 * HD] += times(beside(kv[rows, HD:]), doubled(state.T))
        dlocal[rows, 2 * HD :] += times(beside(kv[rows, :HD]), doubled(state))


def scan_kernel(core, pieces, sums):
    devices = pieces.shape[0]
    flip = core[0] == 1
    total = jnp.zeros(pieces.shape[1:], F32)
    for step in range(devices):
        source = jnp.where(flip, devices - 1 - step, step)
        sums[source] = total
        total += pieces[source]


def joined(back, which, states):
    chips, piece = back.shape[0] // CORES, back.shape[1]
    for chip in range(chips):
        states[which, chip * piece : (chip + 1) * piece, :] = back[CORES * chip + which]
    return states[which]


def dproj_kernel(scale, back, kv, cotangent, dlocal, dproj, states):
    before, after = joined(back, 0, states), joined(back, 1, states)
    prefix, suffix, turned = doubled(before.T), doubled(after), doubled(after.T)
    for rows in chunks(kv.shape[0]):
        for j, term in enumerate(
            (
                times(beside(cotangent[rows, :]), prefix),
                times(beside(kv[rows, HD:]), turned),
                times(beside(kv[rows, :HD]), suffix),
            )
        ):
            columns = slice(j * HD, (j + 1) * HD)
            dproj[rows, columns] = (scale * (dlocal[rows, columns] + term)).astype(BF16)


def attended_kernel(scale, back, query, kv, attended, states):
    state = joined(back, 0, states)
    mask = causal()
    for rows in chunks(query.shape[0]):
        keys, values = kv[rows, :HD], kv[rows, HD:]
        queries = beside(query[rows, :])
        scores = jnp.where(mask, cross(queries, keys), 0.0)
        attended[rows, :] = scale * (
            times(beside(scores), doubled(values)) + times(queries, doubled(state))
        )
        state += gram(beside(keys), beside(values))


def own_kernel(turned, dproj, taken, product, held, sems):
    loads = fetched(taken, held, sems)
    for rows in chunks(turned.shape[0]):
        product[rows, :] = mxu(turned[rows, :], dproj[...])
    for load in loads:
        load.wait()


def total_kernel(turned, dproj, product, total, rows_out, sems):
    stores = []
    for index, rows in enumerate(chunks(turned.shape[0])):
        rows_out[rows, :] = (product[rows, :] + mxu(turned[rows, :], dproj[...])).astype(BF16)
        stores.append(pltpu.make_async_copy(rows_out.at[rows, :], total.at[rows, :], sems.at[index]))
        stores[-1].start()
    for store in stores:
        store.wait()


def sum_kernel(scale, landed, grad):
    total = landed[0].astype(F32)
    for chip in range(1, landed.shape[0]):
        total += landed[chip].astype(F32)
    grad[...] = scale * total


def local(hidden, qkv_weight, out_grad):
    tokens, width = hidden.shape
    group, columns = qkv_weight.shape
    chips = lax.axis_size("chip")
    devices = chips * CORES
    piece = HD // chips
    total_tokens = tokens * devices
    scale = float(HD * total_tokens) ** (-0.5)
    grad_scale = float(total_tokens) ** (-0.5)
    core = lax.axis_index("core").astype(jnp.int32).reshape(1)
    half = width // CORES
    square = tokens * HD * HD
    states = [pltpu.VMEM((2, HD, HD), F32)]

    (copies,) = call(
        spread_kernel, [vmem((chips, group, columns), BF16)], [qkv_weight], 1024, 8, [VMEM]
    )
    mine = lax.all_to_all(copies, "chip", 0, 0, tiled=True)
    keep, give, head = call(
        turn_kernel,
        [hbm((chips, group, tokens), BF16)] * 2 + [vmem((tokens // 2, width), BF16)],
        [core, hidden],
        tokens * width * 1024,
        24,
        [SMEM, VMEM],
    )
    mine, keep, give, head = lax.optimization_barrier((mine, keep, give, head))
    keep, give = keep.reshape(half, tokens), give.reshape(half, tokens)
    taken = lax.ppermute(give, "core", SWAP)
    other = lax.ppermute(mine, "core", SWAP)

    query, kv, parts = call(
        project_kernel,
        [direct((tokens, HD)), direct((tokens, 2 * HD)), vmem((devices, piece, HD))],
        [core, hidden, head, mine, other, out_grad],
        2 * tokens * width * columns + 16 * square,
        32,
        [SMEM, HBM, VMEM, VMEM, VMEM, VMEM],
        [
            pltpu.VMEM((tokens // 2, width), BF16),
            pltpu.VMEM((devices, group, columns), BF16),
            pltpu.VMEM((tokens, columns), F32),
            pltpu.SemaphoreType.DMA(()),
            pltpu.SemaphoreType.DMA((tokens // BLOCK, 2)),
        ],
    )
    pieces = lax.all_to_all(parts, CTX, 0, 0, tiled=True)
    (dlocal,) = call(
        local_kernel,
        [vmem((tokens, columns))],
        [query, kv, out_grad],
        15 * 6 * square,
        24,
        [VMEM] * 3,
    )
    pieces, dlocal = lax.optimization_barrier((pieces, dlocal))
    (sums,) = call(
        scan_kernel, [vmem(parts.shape)], [core, pieces], devices * HD * HD, 8, [SMEM, VMEM]
    )
    back = lax.all_to_all(sums, CTX, 0, 0, tiled=True)

    (dproj,) = call(
        functools.partial(dproj_kernel, scale),
        [vmem((tokens, columns), BF16)],
        [back, kv, out_grad, dlocal],
        24 * square,
        24,
        [VMEM] * 4,
        states,
    )
    theirs = lax.ppermute(dproj, "core", SWAP)
    product, held = call(
        own_kernel,
        [vmem((half, columns)), (pltpu.VMEM((half, tokens), BF16), VMEM)],
        [keep, dproj, taken],
        2 * half * tokens * columns,
        24,
        [VMEM, VMEM, HBM],
        [pltpu.SemaphoreType.DMA((half // BLOCK,))],
    )
    (total,) = call(
        total_kernel,
        [direct((half, columns), BF16)],
        [held, theirs, product],
        2 * half * tokens * columns,
        24,
        [VMEM] * 3,
        [pltpu.VMEM((half, columns), BF16), pltpu.SemaphoreType.DMA((half // BLOCK,))],
    )
    landed = lax.all_to_all(total.reshape(chips, group, columns), "chip", 0, 0, tiled=True)
    (attended,) = call(
        functools.partial(attended_kernel, scale),
        [hbm((tokens, HD))],
        [back, query, kv],
        6 * 6 * square,
        24,
        [VMEM] * 3,
        states,
    )
    (grad,) = call(
        functools.partial(sum_kernel, grad_scale),
        [hbm((group, columns))],
        [landed],
        half * columns,
        16,
        [VMEM],
    )
    return attended, grad


def solution(mesh):
    chips, heads = mesh.shape["ctx"] // CORES, mesh.shape["head"]
    fine = Mesh(mesh.devices.reshape(chips, CORES, heads), ("chip", "core", "head"))
    return jax.shard_map(
        local,
        mesh=fine,
        in_specs=(P(CTX, None), P(CTX, "head"), P(CTX, "head")),
        out_specs=(P(CTX, "head"), P(CTX, "head")),
        check_vma=False,
    )
```

```python
import functools

import jax
import jax.numpy as jnp
from jax import lax
from jax.experimental import pallas as pl
from jax.experimental.pallas import tpu as pltpu
from jax.sharding import Mesh, PartitionSpec as P

HD = 128
BLOCK = 256
CORES = 2
MIB = 1 << 20

SWAP = [(0, 1), (1, 0)]
CTX = ("chip", "core")
RANKS = ("core", "chip")
F32 = jnp.float32
BF16 = jnp.bfloat16

PLAIN = (((1,), (0,)), ((), ()))
ROWS = (((1,), (1,)), ((), ()))
COLS = (((0,), (0,)), ((), ()))


def mxu(a, b, dims=PLAIN):
    return lax.dot_general(a, b, dims, preferred_element_type=F32)


def split(x):
    high = x.astype(BF16)
    return high, (x - high.astype(F32)).astype(BF16)


def beside(x):
    return jnp.concatenate(split(x), axis=1)


def doubled(x):
    both = beside(x)
    return jnp.concatenate([both, both], axis=0)


def folded(out):
    width = out.shape[1] // 2
    return out[:, :width] + out[:, width:]


def times(left, right):
    return folded(mxu(left, right))


def gram(left, right):
    out = folded(mxu(left, right, COLS))
    height = out.shape[0] // 2
    return out[:height] + out[height:]


def cross(left, right):
    high, low = split(right)
    return mxu(left, jnp.concatenate([high, high], axis=1), ROWS) + mxu(
        left, jnp.concatenate([low, low], axis=1), ROWS
    )


HBM = pl.BlockSpec(memory_space=pltpu.HBM)
VMEM = pl.BlockSpec(memory_space=pltpu.VMEM)
SMEM = pl.BlockSpec(memory_space=pltpu.SMEM)


def vmem(dims, dtype=F32):
    return jax.ShapeDtypeStruct(dims, dtype), VMEM


def hbm(dims, dtype=F32):
    return pltpu.HBM(dims, dtype), VMEM


def direct(dims, dtype=F32):
    return pltpu.HBM(dims, dtype), HBM


def call(body, outs, args, flops, limit, specs, scratch=()):
    size = sum(a.size * a.dtype.itemsize for a in args)
    args = [
        pltpu.with_memory_space_constraint(a, pltpu.HBM) if spec is HBM else a
        for a, spec in zip(args, specs)
    ]
    return pl.pallas_call(
        body,
        out_shape=[kind for kind, _ in outs],
        in_specs=specs,
        out_specs=[spec for _, spec in outs],
        scratch_shapes=list(scratch),
        cost_estimate=pl.CostEstimate(flops=flops, bytes_accessed=size, transcendentals=0),
        compiler_params=pltpu.CompilerParams(vmem_limit_bytes=limit * MIB),
    )(*args)


def chunks(total):
    return [slice(start, start + BLOCK) for start in range(0, total, BLOCK)]


def fetched(source, target, sems):
    loads = [
        pltpu.make_async_copy(source.at[rows, :], target.at[rows, :], sems.at[index])
        for index, rows in enumerate(chunks(source.shape[0]))
    ]
    for load in loads:
        load.start()
    return loads


def causal():
    at = lax.broadcasted_iota(jnp.int32, (BLOCK, BLOCK), 0)
    return at >= lax.broadcasted_iota(jnp.int32, (BLOCK, BLOCK), 1)


def spread_kernel(weight, copies):
    for chip in range(copies.shape[0]):
        copies[chip] = weight[...]


def turn_kernel(core, hidden, keep, give, head):
    head[...] = hidden[: head.shape[0], :]
    first = core[0] == 0
    group = keep.shape[1]
    for column in range(hidden.shape[1] // HD):
        turned = hidden[:, column * HD : (column + 1) * HD].T
        for pair in range(HD // (CORES * group)):
            at = pair * CORES * group
            even = turned[at : at + group]
            odd = turned[at + group : at + CORES * group]
            chip = column * (HD // (CORES * group)) + pair
            keep[chip] = jnp.where(first, even, odd)
            give[chip] = jnp.where(first, odd, even)


def project_kernel(core, hidden, head, mine, other, cotangent, query, kv, parts,
                   tail, weight, proj, load_sem, sems):
    ahead = head.shape[0]
    load = pltpu.make_async_copy(hidden.at[ahead:, :], tail, load_sem)
    load.start()
    stores = []
    place = core[0]
    chips, group, columns = mine.shape
    for chip in range(chips):
        for member, held in ((place, mine), (1 - place, other)):
            at = pl.multiple_of((CORES * chip + member) * group, group)
            weight[pl.ds(at, group), :] = held[chip]
    for base, held in ((0, head), (ahead, tail)):
        if base:
            load.wait()
        for rows in chunks(ahead):
            proj[base + rows.start : base + rows.stop, :] = mxu(held[rows, :], weight[...])
        to = pl.ds(base, ahead)
        for which, target, columns_of in ((0, query, pl.ds(0, HD)), (1, kv, pl.ds(HD, 2 * HD))):
            stores.append(
                pltpu.make_async_copy(
                    proj.at[to, columns_of], target.at[to, :], sems.at[len(stores) // 2, which]
                )
            )
            stores[-1].start()
    kv_state = jnp.zeros((HD, HD), F32)
    qg_state = jnp.zeros((HD, HD), F32)
    for rows in chunks(proj.shape[0]):
        part = proj[rows, :]
        kv_state += gram(beside(part[:, HD : 2 * HD]), beside(part[:, 2 * HD :]))
        qg_state += gram(beside(part[:, :HD]), beside(cotangent[rows, :]))
    piece = HD // chips
    for chip in range(chips):
        parts[chip] = kv_state[chip * piece : (chip + 1) * piece]
        parts[chips + chip] = qg_state[chip * piece : (chip + 1) * piece]
    for store in stores:
        store.wait()


def local_kernel(query, kv, cotangent, dlocal):
    mask = causal()
    order = chunks(query.shape[0])
    state = jnp.zeros((HD, HD), F32)
    for rows in order:
        keys, values = kv[rows, :HD], kv[rows, HD:]
        queries, cot = beside(query[rows, :]), beside(cotangent[rows, :])
        scores = jnp.where(mask, cross(queries, keys), 0.0)
        dmat = jnp.where(mask, cross(cot, values), 0.0)
        dquery = times(beside(dmat), doubled(keys))
        if rows is not order[0]:
            dquery += times(cot, doubled(state.T))
        dlocal[rows, 0:HD] = dquery
        dlocal[rows, HD : 2 * HD] = gram(beside(dmat), queries)
        dlocal[rows, 2 * HD :] = gram(beside(scores), cot)
        if rows is not order[-1]:
            state += gram(beside(keys), beside(values))
    state = jnp.zeros((HD, HD), F32)
    for later, rows in zip(order[:0:-1], order[-2::-1]):
        state += gram(beside(query[later, :]), beside(cotangent[later, :]))
        dlocal[rows, HD : 2 * HD] += times(beside(kv[rows, HD:]), doubled(state.T))
        dlocal[rows, 2 * HD :] += times(beside(kv[rows, :HD]), doubled(state))


def scan_kernel(core, pieces, sums):
    devices = pieces.shape[0]
    flip = core[0] == 1
    total = jnp.zeros(pieces.shape[1:], F32)
    rank = [(slab % CORES) * (devices // CORES) + slab // CORES for slab in range(devices)]
    for step in range(devices):
        source = jnp.where(flip, rank[devices - 1 - step], rank[step])
        sums[source] = total
        total += pieces[source]


def joined(back, which, states):
    chips, piece = back.shape[0] // CORES, back.shape[1]
    for chip in range(chips):
        states[which, chip * piece : (chip + 1) * piece, :] = back[which * chips + chip]
    return states[which]


def dproj_kernel(scale, back, kv, cotangent, dlocal, dproj, states):
    before, after = joined(back, 0, states), joined(back, 1, states)
    prefix, suffix, turned = doubled(before.T), doubled(after), doubled(after.T)
    for rows in chunks(kv.shape[0]):
        for j, term in enumerate(
            (
                times(beside(cotangent[rows, :]), prefix),
                times(beside(kv[rows, HD:]), turned),
                times(beside(kv[rows, :HD]), suffix),
            )
        ):
            columns = slice(j * HD, (j + 1) * HD)
            dproj[rows, columns] = (scale * (dlocal[rows, columns] + term)).astype(BF16)


def attended_kernel(scale, back, query, kv, attended, states):
    state = joined(back, 0, states)
    mask = causal()
    for rows in chunks(query.shape[0]):
        keys, values = kv[rows, :HD], kv[rows, HD:]
        queries = beside(query[rows, :])
        scores = jnp.where(mask, cross(queries, keys), 0.0)
        attended[rows, :] = scale * (
            times(beside(scores), doubled(values)) + times(queries, doubled(state))
        )
        state += gram(beside(keys), beside(values))


def own_kernel(turned, dproj, taken, product, held, sems):
    loads = fetched(taken, held, sems)
    for rows in chunks(turned.shape[0]):
        product[rows, :] = mxu(turned[rows, :], dproj[...])
    for load in loads:
        load.wait()


def total_kernel(turned, dproj, product, total, rows_out, sems):
    stores = []
    for index, rows in enumerate(chunks(turned.shape[0])):
        rows_out[rows, :] = (product[rows, :] + mxu(turned[rows, :], dproj[...])).astype(BF16)
        stores.append(pltpu.make_async_copy(rows_out.at[rows, :], total.at[rows, :], sems.at[index]))
        stores[-1].start()
    for store in stores:
        store.wait()


def sum_kernel(scale, landed, grad):
    total = landed[0].astype(F32)
    for chip in range(1, landed.shape[0]):
        total += landed[chip].astype(F32)
    grad[...] = scale * total


def local(hidden, qkv_weight, out_grad):
    tokens, width = hidden.shape
    group, columns = qkv_weight.shape
    chips = lax.axis_size("chip")
    devices = chips * CORES
    piece = HD // chips
    total_tokens = tokens * devices
    scale = float(HD * total_tokens) ** (-0.5)
    grad_scale = float(total_tokens) ** (-0.5)
    core = lax.axis_index("core").astype(jnp.int32).reshape(1)
    half = width // CORES
    square = tokens * HD * HD
    states = [pltpu.VMEM((2, HD, HD), F32)]

    (copies,) = call(
        spread_kernel, [vmem((chips, group, columns), BF16)], [qkv_weight], 1024, 8, [VMEM]
    )
    mine = lax.all_to_all(copies, "chip", 0, 0, tiled=True)
    keep, give, head = call(
        turn_kernel,
        [hbm((chips, group, tokens), BF16)] * 2 + [vmem((tokens // 2, width), BF16)],
        [core, hidden],
        tokens * width * 1024,
        24,
        [SMEM, VMEM],
    )
    mine, keep, give, head = lax.optimization_barrier((mine, keep, give, head))
    keep, give = keep.reshape(half, tokens), give.reshape(half, tokens)
    taken = lax.ppermute(give, "core", SWAP)
    other = lax.ppermute(mine, "core", SWAP)

    query, kv, parts = call(
        project_kernel,
        [direct((tokens, HD)), direct((tokens, 2 * HD)), vmem((devices, piece, HD))],
        [core, hidden, head, mine, other, out_grad],
        2 * tokens * width * columns + 16 * square,
        32,
        [SMEM, HBM, VMEM, VMEM, VMEM, VMEM],
        [
            pltpu.VMEM((tokens // 2, width), BF16),
            pltpu.VMEM((width, columns), BF16),
            pltpu.VMEM((tokens, columns), F32),
            pltpu.SemaphoreType.DMA(()),
            pltpu.SemaphoreType.DMA((2, 2)),
        ],
    )
    pieces = lax.all_to_all(parts, RANKS, 0, 0, tiled=True)
    (dlocal,) = call(
        local_kernel,
        [vmem((tokens, columns))],
        [query, kv, out_grad],
        15 * 6 * square,
        24,
        [VMEM] * 3,
    )
    pieces, dlocal = lax.optimization_barrier((pieces, dlocal))
    (sums,) = call(
        scan_kernel, [vmem(parts.shape)], [core, pieces], devices * HD * HD, 8, [SMEM, VMEM]
    )
    back = lax.all_to_all(sums, RANKS, 0, 0, tiled=True)

    (dproj,) = call(
        functools.partial(dproj_kernel, scale),
        [vmem((tokens, columns), BF16)],
        [back, kv, out_grad, dlocal],
        24 * square,
        24,
        [VMEM] * 4,
        states,
    )
    theirs = lax.ppermute(dproj, "core", SWAP)
    product, held = call(
        own_kernel,
        [vmem((half, columns)), (pltpu.VMEM((half, tokens), BF16), VMEM)],
        [keep, dproj, taken],
        2 * half * tokens * columns,
        24,
        [VMEM, VMEM, HBM],
        [pltpu.SemaphoreType.DMA((half // BLOCK,))],
    )
    (total,) = call(
        total_kernel,
        [direct((half, columns), BF16)],
        [held, theirs, product],
        2 * half * tokens * columns,
        24,
        [VMEM] * 3,
        [pltpu.VMEM((half, columns), BF16), pltpu.SemaphoreType.DMA((half // BLOCK,))],
    )
    landed = lax.all_to_all(total.reshape(chips, group, columns), "chip", 0, 0, tiled=True)
    (attended,) = call(
        functools.partial(attended_kernel, scale),
        [hbm((tokens, HD))],
        [back, query, kv],
        6 * 6 * square,
        24,
        [VMEM] * 3,
        states,
    )
    (grad,) = call(
        functools.partial(sum_kernel, grad_scale),
        [hbm((group, columns))],
        [landed],
        half * columns,
        16,
        [VMEM],
    )
    return attended, grad


def solution(mesh):
    chips, heads = mesh.shape["ctx"] // CORES, mesh.shape["head"]
    fine = Mesh(mesh.devices.reshape(chips, CORES, heads), ("chip", "core", "head"))
    return jax.shard_map(
        local,
        mesh=fine,
        in_specs=(P(CTX, None), P(CTX, "head"), P(CTX, "head")),
        out_specs=(P(CTX, "head"), P(CTX, "head")),
        check_vma=False,
    )
```

```python
import functools

import jax
import jax.numpy as jnp
from jax import lax
from jax.experimental import pallas as pl
from jax.experimental.pallas import tpu as pltpu
from jax.sharding import Mesh, PartitionSpec as P

HD = 128
BLOCK = 256
PARTS = 4
CORES = 2
MIB = 1 << 20

SWAP = [(0, 1), (1, 0)]
CTX = ("chip", "core")
RANKS = ("core", "chip")
F32 = jnp.float32
BF16 = jnp.bfloat16

PLAIN = (((1,), (0,)), ((), ()))
ROWS = (((1,), (1,)), ((), ()))
COLS = (((0,), (0,)), ((), ()))


def mxu(a, b, dims=PLAIN):
    return lax.dot_general(a, b, dims, preferred_element_type=F32)


def split(x):
    high = x.astype(BF16)
    return high, (x - high.astype(F32)).astype(BF16)


def beside(x):
    return jnp.concatenate(split(x), axis=1)


def doubled(x):
    both = beside(x)
    return jnp.concatenate([both, both], axis=0)


def folded(out):
    width = out.shape[1] // 2
    return out[:, :width] + out[:, width:]


def times(left, right):
    return folded(mxu(left, right))


def gram(left, right):
    out = folded(mxu(left, right, COLS))
    height = out.shape[0] // 2
    return out[:height] + out[height:]


def cross(left, right):
    high, low = split(right)
    return mxu(left, jnp.concatenate([high, high], axis=1), ROWS) + mxu(
        left, jnp.concatenate([low, low], axis=1), ROWS
    )


HBM = pl.BlockSpec(memory_space=pltpu.HBM)
VMEM = pl.BlockSpec(memory_space=pltpu.VMEM)
SMEM = pl.BlockSpec(memory_space=pltpu.SMEM)


def vmem(dims, dtype=F32):
    return jax.ShapeDtypeStruct(dims, dtype), VMEM


def hbm(dims, dtype=F32):
    return pltpu.HBM(dims, dtype), VMEM


def direct(dims, dtype=F32):
    return pltpu.HBM(dims, dtype), HBM


def call(body, outs, args, flops, limit, specs, scratch=()):
    size = sum(a.size * a.dtype.itemsize for a in args)
    args = [
        pltpu.with_memory_space_constraint(a, pltpu.HBM) if spec is HBM else a
        for a, spec in zip(args, specs)
    ]
    return pl.pallas_call(
        body,
        out_shape=[kind for kind, _ in outs],
        in_specs=specs,
        out_specs=[spec for _, spec in outs],
        scratch_shapes=list(scratch),
        cost_estimate=pl.CostEstimate(flops=flops, bytes_accessed=size, transcendentals=0),
        compiler_params=pltpu.CompilerParams(vmem_limit_bytes=limit * MIB),
    )(*args)


def chunks(total):
    return [slice(start, start + BLOCK) for start in range(0, total, BLOCK)]


def causal():
    at = lax.broadcasted_iota(jnp.int32, (BLOCK, BLOCK), 0)
    return at >= lax.broadcasted_iota(jnp.int32, (BLOCK, BLOCK), 1)


def spread_kernel(weight, copies):
    for chip in range(copies.shape[0]):
        copies[chip] = weight[...]


def prepare_kernel(group, core, hidden, near, far, keep, *give):
    wide = 2 * HD
    at = lax.broadcasted_iota(jnp.int32, (wide, wide), 0)
    to = lax.broadcasted_iota(jnp.int32, (wide, wide), 1)
    parity = jnp.where(to < HD, core[0], 1 - core[0])
    slot = lax.rem(to, HD)
    source = (lax.div(slot, group) * CORES + parity) * group + lax.rem(slot, group)
    order = jnp.where(at == source, 1.0, 0.0).astype(BF16)
    for step in range(hidden.shape[1] // wide):
        columns = mxu(hidden[:, step * wide : (step + 1) * wide], order).astype(BF16)
        span = slice(step * HD, (step + 1) * HD)
        near[:, span] = columns[:, :HD]
        far[:, span] = columns[:, HD:]
        keep[span, :] = columns[:, :HD].T
        which, first = divmod(step * HD, give[0].shape[0])
        give[which][first : first + HD, :] = columns[:, HD:].T


def half_kernel(near, mine, partial):
    chips, group, columns = mine.shape
    for rows in chunks(near.shape[0]):
        partial[rows, :] = mxu(near[rows, :], mine[...].reshape(chips * group, columns))


def project_kernel(far, other, partial, cotangent, query, kv, parts, proj, sems):
    chips, group, columns = other.shape
    stores = []
    for rows in chunks(far.shape[0]):
        weight = other[...].reshape(chips * group, columns)
        proj[rows, :] = partial[rows, :] + mxu(far[rows, :], weight)
        for which, target, span in ((0, query, pl.ds(0, HD)), (1, kv, pl.ds(HD, 2 * HD))):
            stores.append(
                pltpu.make_async_copy(
                    proj.at[rows, span], target.at[rows, :], sems.at[len(stores) // 2, which]
                )
            )
            stores[-1].start()
    kv_state = jnp.zeros((HD, HD), F32)
    qg_state = jnp.zeros((HD, HD), F32)
    for rows in chunks(proj.shape[0]):
        part = proj[rows, :]
        kv_state += gram(beside(part[:, HD : 2 * HD]), beside(part[:, 2 * HD :]))
        qg_state += gram(beside(part[:, :HD]), beside(cotangent[rows, :]))
    piece = HD // chips
    for chip in range(chips):
        parts[chip] = kv_state[chip * piece : (chip + 1) * piece]
        parts[chips + chip] = qg_state[chip * piece : (chip + 1) * piece]
    for store in stores:
        store.wait()


def local_kernel(query, kv, cotangent, dlocal):
    mask = causal()
    order = chunks(query.shape[0])
    state = jnp.zeros((HD, HD), F32)
    for rows in order:
        keys, values = kv[rows, :HD], kv[rows, HD:]
        queries, cot = beside(query[rows, :]), beside(cotangent[rows, :])
        scores = jnp.where(mask, cross(queries, keys), 0.0)
        dmat = jnp.where(mask, cross(cot, values), 0.0)
        dquery = times(beside(dmat), doubled(keys))
        if rows is not order[0]:
            dquery += times(cot, doubled(state.T))
        dlocal[rows, 0:HD] = dquery
        dlocal[rows, HD : 2 * HD] = gram(beside(dmat), queries)
        dlocal[rows, 2 * HD :] = gram(beside(scores), cot)
        if rows is not order[-1]:
            state += gram(beside(keys), beside(values))
    state = jnp.zeros((HD, HD), F32)
    for later, rows in zip(order[:0:-1], order[-2::-1]):
        state += gram(beside(query[later, :]), beside(cotangent[later, :]))
        dlocal[rows, HD : 2 * HD] += times(beside(kv[rows, HD:]), doubled(state.T))
        dlocal[rows, 2 * HD :] += times(beside(kv[rows, :HD]), doubled(state))


def scan_kernel(core, pieces, sums):
    devices = pieces.shape[0]
    flip = core[0] == 1
    total = jnp.zeros(pieces.shape[1:], F32)
    rank = [(slab % CORES) * (devices // CORES) + slab // CORES for slab in range(devices)]
    for step in range(devices):
        source = jnp.where(flip, rank[devices - 1 - step], rank[step])
        sums[source] = total
        total += pieces[source]


def joined(back, which, states):
    chips, piece = back.shape[0] // CORES, back.shape[1]
    for chip in range(chips):
        states[which, chip * piece : (chip + 1) * piece, :] = back[which * chips + chip]
    return states[which]


def dproj_kernel(scale, back, kv, cotangent, dlocal, dproj, states):
    before, after = joined(back, 0, states), joined(back, 1, states)
    prefix, suffix, turned = doubled(before.T), doubled(after), doubled(after.T)
    for rows in chunks(kv.shape[0]):
        for j, term in enumerate(
            (
                times(beside(cotangent[rows, :]), prefix),
                times(beside(kv[rows, HD:]), turned),
                times(beside(kv[rows, :HD]), suffix),
            )
        ):
            columns = slice(j * HD, (j + 1) * HD)
            dproj[rows, columns] = (scale * (dlocal[rows, columns] + term)).astype(BF16)


def attended_kernel(scale, back, query, kv, attended, states):
    state = joined(back, 0, states)
    mask = causal()
    for rows in chunks(query.shape[0]):
        keys, values = kv[rows, :HD], kv[rows, HD:]
        queries = beside(query[rows, :])
        scores = jnp.where(mask, cross(queries, keys), 0.0)
        attended[rows, :] = scale * (
            times(beside(scores), doubled(values)) + times(queries, doubled(state))
        )
        state += gram(beside(keys), beside(values))


def own_kernel(turned, dproj, *refs):
    taken, (product, held, sems) = refs[:PARTS], refs[PARTS:]
    size = taken[0].shape[0]
    loads = [
        pltpu.make_async_copy(part, held.at[index * size : (index + 1) * size, :], sems.at[index])
        for index, part in enumerate(taken)
    ]
    for load in loads:
        load.start()
    for rows in chunks(turned.shape[0]):
        product[rows, :] = mxu(turned[rows, :], dproj[...])
    for load in loads:
        load.wait()


def total_kernel(turned, dproj, product, total, rows_out, sems):
    stores = []
    for index, rows in enumerate(chunks(turned.shape[0])):
        rows_out[rows, :] = (product[rows, :] + mxu(turned[rows, :], dproj[...])).astype(BF16)
        stores.append(pltpu.make_async_copy(rows_out.at[rows, :], total.at[rows, :], sems.at[index]))
        stores[-1].start()
    for store in stores:
        store.wait()


def sum_kernel(scale, landed, grad):
    total = landed[0].astype(F32)
    for chip in range(1, landed.shape[0]):
        total += landed[chip].astype(F32)
    grad[...] = scale * total


def local(hidden, qkv_weight, out_grad):
    tokens, width = hidden.shape
    group, columns = qkv_weight.shape
    chips = lax.axis_size("chip")
    devices = chips * CORES
    piece = HD // chips
    total_tokens = tokens * devices
    scale = float(HD * total_tokens) ** (-0.5)
    grad_scale = float(total_tokens) ** (-0.5)
    core = lax.axis_index("core").astype(jnp.int32).reshape(1)
    half = width // CORES
    square = tokens * HD * HD
    states = [pltpu.VMEM((2, HD, HD), F32)]

    (copies,) = call(
        spread_kernel, [vmem((chips, group, columns), BF16)], [qkv_weight], 1024, 8, [VMEM]
    )
    mine = lax.all_to_all(copies, "chip", 0, 0, tiled=True)
    near, far, keep, *give = call(
        functools.partial(prepare_kernel, group),
        [
            vmem((tokens, half), BF16),
            hbm((tokens, half), BF16),
            hbm((half, tokens), BF16),
        ]
        + [hbm((half // PARTS, tokens), BF16)] * PARTS,
        [core, hidden],
        tokens * width * 1024,
        24,
        [SMEM, VMEM],
    )
    taken = [lax.ppermute(part, "core", SWAP) for part in give]
    mine, near, far, keep, taken = lax.optimization_barrier((mine, near, far, keep, taken))
    other = lax.ppermute(mine, "core", SWAP)
    (partial,) = call(
        half_kernel,
        [vmem((tokens, columns))],
        [near, mine],
        2 * tokens * half * columns,
        16,
        [VMEM, VMEM],
    )
    query, kv, parts = call(
        project_kernel,
        [direct((tokens, HD)), direct((tokens, 2 * HD)), vmem((devices, piece, HD))],
        [far, other, partial, out_grad],
        2 * tokens * half * columns + 16 * square,
        24,
        [VMEM] * 4,
        [
            pltpu.VMEM((tokens, columns), F32),
            pltpu.SemaphoreType.DMA((tokens // BLOCK, 2)),
        ],
    )
    pieces = lax.all_to_all(parts, RANKS, 0, 0, tiled=True)
    (dlocal,) = call(
        local_kernel,
        [vmem((tokens, columns))],
        [query, kv, out_grad],
        15 * 6 * square,
        24,
        [VMEM] * 3,
    )
    pieces, dlocal = lax.optimization_barrier((pieces, dlocal))
    (sums,) = call(
        scan_kernel, [vmem(parts.shape)], [core, pieces], devices * HD * HD, 8, [SMEM, VMEM]
    )
    back = lax.all_to_all(sums, RANKS, 0, 0, tiled=True)

    (dproj,) = call(
        functools.partial(dproj_kernel, scale),
        [vmem((tokens, columns), BF16)],
        [back, kv, out_grad, dlocal],
        24 * square,
        24,
        [VMEM] * 4,
        states,
    )
    theirs = lax.ppermute(dproj, "core", SWAP)
    product, held = call(
        own_kernel,
        [vmem((half, columns)), (pltpu.VMEM((half, tokens), BF16), VMEM)],
        [keep, dproj, *taken],
        2 * half * tokens * columns,
        24,
        [VMEM, VMEM] + [HBM] * PARTS,
        [pltpu.SemaphoreType.DMA((PARTS,))],
    )
    (total,) = call(
        total_kernel,
        [direct((half, columns), BF16)],
        [held, theirs, product],
        2 * half * tokens * columns,
        24,
        [VMEM] * 3,
        [pltpu.VMEM((half, columns), BF16), pltpu.SemaphoreType.DMA((half // BLOCK,))],
    )
    landed = lax.all_to_all(total.reshape(chips, group, columns), "chip", 0, 0, tiled=True)
    (attended,) = call(
        functools.partial(attended_kernel, scale),
        [hbm((tokens, HD))],
        [back, query, kv],
        6 * 6 * square,
        24,
        [VMEM] * 3,
        states,
    )
    (grad,) = call(
        functools.partial(sum_kernel, grad_scale),
        [hbm((group, columns))],
        [landed],
        half * columns,
        16,
        [VMEM],
    )
    return attended, grad


def solution(mesh):
    chips, heads = mesh.shape["ctx"] // CORES, mesh.shape["head"]
    fine = Mesh(mesh.devices.reshape(chips, CORES, heads), ("chip", "core", "head"))
    return jax.shard_map(
        local,
        mesh=fine,
        in_specs=(P(CTX, None), P(CTX, "head"), P(CTX, "head")),
        out_specs=(P(CTX, "head"), P(CTX, "head")),
        check_vma=False,
    )
```

```python
import functools

import jax
import jax.numpy as jnp
from jax import lax
from jax.experimental import pallas as pl
from jax.experimental.pallas import tpu as pltpu
from jax.sharding import Mesh, PartitionSpec as P

HD = 128
BLOCK = 256
PARTS = 4
CORES = 2
MIB = 1 << 20

SWAP = [(0, 1), (1, 0)]
CTX = ("chip", "core")
RANKS = ("core", "chip")
F32 = jnp.float32
BF16 = jnp.bfloat16

PLAIN = (((1,), (0,)), ((), ()))
ROWS = (((1,), (1,)), ((), ()))
COLS = (((0,), (0,)), ((), ()))


def mxu(a, b, dims=PLAIN):
    return lax.dot_general(a, b, dims, preferred_element_type=F32)


def split(x):
    high = x.astype(BF16)
    return high, (x - high.astype(F32)).astype(BF16)


def beside(x):
    return jnp.concatenate(split(x), axis=1)


def doubled(x):
    both = beside(x)
    return jnp.concatenate([both, both], axis=0)


def folded(out):
    width = out.shape[1] // 2
    return out[:, :width] + out[:, width:]


def times(left, right):
    return folded(mxu(left, right))


def gram(left, right):
    out = folded(mxu(left, right, COLS))
    height = out.shape[0] // 2
    return out[:height] + out[height:]


def cross(left, right):
    high, low = split(right)
    return mxu(left, jnp.concatenate([high, high], axis=1), ROWS) + mxu(
        left, jnp.concatenate([low, low], axis=1), ROWS
    )


HBM = pl.BlockSpec(memory_space=pltpu.HBM)
VMEM = pl.BlockSpec(memory_space=pltpu.VMEM)
SMEM = pl.BlockSpec(memory_space=pltpu.SMEM)


def vmem(dims, dtype=F32):
    return jax.ShapeDtypeStruct(dims, dtype), VMEM


def hbm(dims, dtype=F32):
    return pltpu.HBM(dims, dtype), VMEM


def direct(dims, dtype=F32):
    return pltpu.HBM(dims, dtype), HBM


def call(body, outs, args, flops, limit, specs, scratch=()):
    size = sum(a.size * a.dtype.itemsize for a in args)
    args = [
        pltpu.with_memory_space_constraint(a, pltpu.HBM) if spec is HBM else a
        for a, spec in zip(args, specs)
    ]
    return pl.pallas_call(
        body,
        out_shape=[kind for kind, _ in outs],
        in_specs=specs,
        out_specs=[spec for _, spec in outs],
        scratch_shapes=list(scratch),
        cost_estimate=pl.CostEstimate(flops=flops, bytes_accessed=size, transcendentals=0),
        compiler_params=pltpu.CompilerParams(vmem_limit_bytes=limit * MIB),
    )(*args)


def chunks(total):
    return [slice(start, start + BLOCK) for start in range(0, total, BLOCK)]


def causal():
    at = lax.broadcasted_iota(jnp.int32, (BLOCK, BLOCK), 0)
    return at >= lax.broadcasted_iota(jnp.int32, (BLOCK, BLOCK), 1)


def spread_kernel(weight, copies):
    for chip in range(copies.shape[0]):
        copies[chip] = weight[...]


def prepare_kernel(group, core, hidden, near, far, keep, *give):
    wide = 2 * HD
    at = lax.broadcasted_iota(jnp.int32, (wide, wide), 0)
    to = lax.broadcasted_iota(jnp.int32, (wide, wide), 1)
    parity = jnp.where(to < HD, core[0], 1 - core[0])
    slot = lax.rem(to, HD)
    source = (lax.div(slot, group) * CORES + parity) * group + lax.rem(slot, group)
    order = jnp.where(at == source, 1.0, 0.0).astype(BF16)
    for step in range(hidden.shape[1] // wide):
        columns = mxu(hidden[:, step * wide : (step + 1) * wide], order).astype(BF16)
        span = slice(step * HD, (step + 1) * HD)
        near[:, span] = columns[:, :HD]
        far[:, span] = columns[:, HD:]
        keep[span, :] = columns[:, :HD].T
        which, first = divmod(step * HD, give[0].shape[0])
        give[which][first : first + HD, :] = columns[:, HD:].T


def half_kernel(near, mine, partial):
    chips, group, columns = mine.shape
    for rows in chunks(near.shape[0]):
        partial[rows, :] = mxu(near[rows, :], mine[...].reshape(chips * group, columns))


def project_kernel(far, other, partial, cotangent, query, kv, parts, held, sems):
    chips, group, columns = other.shape
    stores = []
    for rows in chunks(far.shape[0]):
        weight = other[...].reshape(chips * group, columns)
        part = partial[rows, :] + mxu(far[rows, :], weight)
        held[rows, :] = part[:, :HD]
        kv[rows, :] = part[:, HD:]
        stores.append(
            pltpu.make_async_copy(held.at[rows, :], query.at[rows, :], sems.at[len(stores)])
        )
        stores[-1].start()
    kv_state = jnp.zeros((HD, HD), F32)
    qg_state = jnp.zeros((HD, HD), F32)
    for rows in chunks(far.shape[0]):
        kv_state += gram(beside(kv[rows, :HD]), beside(kv[rows, HD:]))
        qg_state += gram(beside(held[rows, :]), beside(cotangent[rows, :]))
    piece = HD // chips
    for chip in range(chips):
        parts[chip] = kv_state[chip * piece : (chip + 1) * piece]
        parts[chips + chip] = qg_state[chip * piece : (chip + 1) * piece]
    for store in stores:
        store.wait()


def local_kernel(query, kv, cotangent, dlocal):
    mask = causal()
    order = chunks(query.shape[0])
    state = jnp.zeros((HD, HD), F32)
    for rows in order:
        keys, values = kv[rows, :HD], kv[rows, HD:]
        queries, cot = beside(query[rows, :]), beside(cotangent[rows, :])
        scores = jnp.where(mask, cross(queries, keys), 0.0)
        dmat = jnp.where(mask, cross(cot, values), 0.0)
        dquery = times(beside(dmat), doubled(keys))
        if rows is not order[0]:
            dquery += times(cot, doubled(state.T))
        dlocal[rows, 0:HD] = dquery
        dlocal[rows, HD : 2 * HD] = gram(beside(dmat), queries)
        dlocal[rows, 2 * HD :] = gram(beside(scores), cot)
        if rows is not order[-1]:
            state += gram(beside(keys), beside(values))
    state = jnp.zeros((HD, HD), F32)
    for later, rows in zip(order[:0:-1], order[-2::-1]):
        state += gram(beside(query[later, :]), beside(cotangent[later, :]))
        dlocal[rows, HD : 2 * HD] += times(beside(kv[rows, HD:]), doubled(state.T))
        dlocal[rows, 2 * HD :] += times(beside(kv[rows, :HD]), doubled(state))


def scan_kernel(core, pieces, sums):
    devices = pieces.shape[0]
    flip = core[0] == 1
    total = jnp.zeros(pieces.shape[1:], F32)
    rank = [(slab % CORES) * (devices // CORES) + slab // CORES for slab in range(devices)]
    for step in range(devices):
        source = jnp.where(flip, rank[devices - 1 - step], rank[step])
        sums[source] = total
        total += pieces[source]


def joined(back, which, states):
    chips, piece = back.shape[0] // CORES, back.shape[1]
    for chip in range(chips):
        states[which, chip * piece : (chip + 1) * piece, :] = back[which * chips + chip]
    return states[which]


def dproj_kernel(scale, back, kv, cotangent, dlocal, dproj, states):
    before, after = joined(back, 0, states), joined(back, 1, states)
    prefix, suffix, turned = doubled(before.T), doubled(after), doubled(after.T)
    for rows in chunks(kv.shape[0]):
        for j, term in enumerate(
            (
                times(beside(cotangent[rows, :]), prefix),
                times(beside(kv[rows, HD:]), turned),
                times(beside(kv[rows, :HD]), suffix),
            )
        ):
            columns = slice(j * HD, (j + 1) * HD)
            dproj[rows, columns] = (scale * (dlocal[rows, columns] + term)).astype(BF16)


def attended_kernel(scale, back, query, kv, attended, states):
    state = joined(back, 0, states)
    mask = causal()
    for rows in chunks(query.shape[0]):
        keys, values = kv[rows, :HD], kv[rows, HD:]
        queries = beside(query[rows, :])
        scores = jnp.where(mask, cross(queries, keys), 0.0)
        attended[rows, :] = scale * (
            times(beside(scores), doubled(values)) + times(queries, doubled(state))
        )
        state += gram(beside(keys), beside(values))


def own_kernel(turned, dproj, *refs):
    taken, (product, held, sems) = refs[:PARTS], refs[PARTS:]
    size = taken[0].shape[0]
    loads = [
        pltpu.make_async_copy(part, held.at[index * size : (index + 1) * size, :], sems.at[index])
        for index, part in enumerate(taken)
    ]
    for load in loads:
        load.start()
    for rows in chunks(turned.shape[0]):
        product[rows, :] = mxu(turned[rows, :], dproj[...])
    for load in loads:
        load.wait()


def total_kernel(turned, dproj, product, total, rows_out, sems):
    stores = []
    for index, rows in enumerate(chunks(turned.shape[0])):
        rows_out[rows, :] = (product[rows, :] + mxu(turned[rows, :], dproj[...])).astype(BF16)
        stores.append(pltpu.make_async_copy(rows_out.at[rows, :], total.at[rows, :], sems.at[index]))
        stores[-1].start()
    for store in stores:
        store.wait()


def sum_kernel(scale, landed, grad):
    total = landed[0].astype(F32)
    for chip in range(1, landed.shape[0]):
        total += landed[chip].astype(F32)
    grad[...] = scale * total


def local(hidden, qkv_weight, out_grad):
    tokens, width = hidden.shape
    group, columns = qkv_weight.shape
    chips = lax.axis_size("chip")
    devices = chips * CORES
    piece = HD // chips
    total_tokens = tokens * devices
    scale = float(HD * total_tokens) ** (-0.5)
    grad_scale = float(total_tokens) ** (-0.5)
    core = lax.axis_index("core").astype(jnp.int32).reshape(1)
    half = width // CORES
    square = tokens * HD * HD
    states = [pltpu.VMEM((2, HD, HD), F32)]

    (copies,) = call(
        spread_kernel, [vmem((chips, group, columns), BF16)], [qkv_weight], 1024, 8, [VMEM]
    )
    mine = lax.all_to_all(copies, "chip", 0, 0, tiled=True)
    near, far, keep, *give = call(
        functools.partial(prepare_kernel, group),
        [
            vmem((tokens, half), BF16),
            hbm((tokens, half), BF16),
            hbm((half, tokens), BF16),
        ]
        + [hbm((half // PARTS, tokens), BF16)] * PARTS,
        [core, hidden],
        tokens * width * 1024,
        24,
        [SMEM, VMEM],
    )
    taken = [lax.ppermute(part, "core", SWAP) for part in give]
    mine, near, far, keep, taken = lax.optimization_barrier((mine, near, far, keep, taken))
    other = lax.ppermute(mine, "core", SWAP)
    (partial,) = call(
        half_kernel,
        [vmem((tokens, columns))],
        [near, mine],
        2 * tokens * half * columns,
        16,
        [VMEM, VMEM],
    )
    query, kv, parts = call(
        project_kernel,
        [direct((tokens, HD)), vmem((tokens, 2 * HD)), vmem((devices, piece, HD))],
        [far, other, partial, out_grad],
        2 * tokens * half * columns + 16 * square,
        24,
        [VMEM] * 4,
        [pltpu.VMEM((tokens, HD), F32), pltpu.SemaphoreType.DMA((tokens // BLOCK,))],
    )
    pieces = lax.all_to_all(parts, RANKS, 0, 0, tiled=True)
    (dlocal,) = call(
        local_kernel,
        [vmem((tokens, columns))],
        [query, kv, out_grad],
        15 * 6 * square,
        24,
        [VMEM] * 3,
    )
    pieces, dlocal = lax.optimization_barrier((pieces, dlocal))
    (sums,) = call(
        scan_kernel, [vmem(parts.shape)], [core, pieces], devices * HD * HD, 8, [SMEM, VMEM]
    )
    back = lax.all_to_all(sums, RANKS, 0, 0, tiled=True)

    (dproj,) = call(
        functools.partial(dproj_kernel, scale),
        [vmem((tokens, columns), BF16)],
        [back, kv, out_grad, dlocal],
        24 * square,
        24,
        [VMEM] * 4,
        states,
    )
    theirs = lax.ppermute(dproj, "core", SWAP)
    product, held = call(
        own_kernel,
        [vmem((half, columns)), (pltpu.VMEM((half, tokens), BF16), VMEM)],
        [keep, dproj, *taken],
        2 * half * tokens * columns,
        24,
        [VMEM, VMEM] + [HBM] * PARTS,
        [pltpu.SemaphoreType.DMA((PARTS,))],
    )
    (total,) = call(
        total_kernel,
        [direct((half, columns), BF16)],
        [held, theirs, product],
        2 * half * tokens * columns,
        24,
        [VMEM] * 3,
        [pltpu.VMEM((half, columns), BF16), pltpu.SemaphoreType.DMA((half // BLOCK,))],
    )
    landed = lax.all_to_all(total.reshape(chips, group, columns), "chip", 0, 0, tiled=True)
    (attended,) = call(
        functools.partial(attended_kernel, scale),
        [hbm((tokens, HD))],
        [back, query, kv],
        6 * 6 * square,
        24,
        [VMEM] * 3,
        states,
    )
    (grad,) = call(
        functools.partial(sum_kernel, grad_scale),
        [hbm((group, columns))],
        [landed],
        half * columns,
        16,
        [VMEM],
    )
    return attended, grad


def solution(mesh):
    chips, heads = mesh.shape["ctx"] // CORES, mesh.shape["head"]
    fine = Mesh(mesh.devices.reshape(chips, CORES, heads), ("chip", "core", "head"))
    return jax.shard_map(
        local,
        mesh=fine,
        in_specs=(P(CTX, None), P(CTX, "head"), P(CTX, "head")),
        out_specs=(P(CTX, "head"), P(CTX, "head")),
        check_vma=False,
    )
```

```python
import functools

import jax
import jax.numpy as jnp
from jax import lax
from jax.experimental import pallas as pl
from jax.experimental.pallas import tpu as pltpu
from jax.sharding import Mesh, PartitionSpec as P

HD = 128
BLOCK = 256
PARTS = 4
CORES = 2
MIB = 1 << 20

SWAP = [(0, 1), (1, 0)]
CTX = ("chip", "core")
RANKS = ("core", "chip")
F32 = jnp.float32
BF16 = jnp.bfloat16

PLAIN = (((1,), (0,)), ((), ()))
ROWS = (((1,), (1,)), ((), ()))
COLS = (((0,), (0,)), ((), ()))


def mxu(a, b, dims=PLAIN):
    return lax.dot_general(a, b, dims, preferred_element_type=F32)


def split(x):
    high = x.astype(BF16)
    return high, (x - high.astype(F32)).astype(BF16)


def beside(x):
    return jnp.concatenate(split(x), axis=1)


def doubled(x):
    both = beside(x)
    return jnp.concatenate([both, both], axis=0)


def folded(out):
    width = out.shape[1] // 2
    return out[:, :width] + out[:, width:]


def times(left, right):
    return folded(mxu(left, right))


def gram(left, right):
    out = folded(mxu(left, right, COLS))
    height = out.shape[0] // 2
    return out[:height] + out[height:]


def cross(left, right):
    high, low = split(right)
    return mxu(left, jnp.concatenate([high, high], axis=1), ROWS) + mxu(
        left, jnp.concatenate([low, low], axis=1), ROWS
    )


HBM = pl.BlockSpec(memory_space=pltpu.HBM)
VMEM = pl.BlockSpec(memory_space=pltpu.VMEM)
SMEM = pl.BlockSpec(memory_space=pltpu.SMEM)


def vmem(dims, dtype=F32):
    return jax.ShapeDtypeStruct(dims, dtype), VMEM


def hbm(dims, dtype=F32):
    return pltpu.HBM(dims, dtype), VMEM


def direct(dims, dtype=F32):
    return pltpu.HBM(dims, dtype), HBM


def call(body, outs, args, flops, limit, specs, scratch=()):
    size = sum(a.size * a.dtype.itemsize for a in args)
    args = [
        pltpu.with_memory_space_constraint(a, pltpu.HBM) if spec is HBM else a
        for a, spec in zip(args, specs)
    ]
    return pl.pallas_call(
        body,
        out_shape=[kind for kind, _ in outs],
        in_specs=specs,
        out_specs=[spec for _, spec in outs],
        scratch_shapes=list(scratch),
        cost_estimate=pl.CostEstimate(flops=flops, bytes_accessed=size, transcendentals=0),
        compiler_params=pltpu.CompilerParams(vmem_limit_bytes=limit * MIB),
    )(*args)


def chunks(total):
    return [slice(start, start + BLOCK) for start in range(0, total, BLOCK)]


def causal():
    at = lax.broadcasted_iota(jnp.int32, (BLOCK, BLOCK), 0)
    return at >= lax.broadcasted_iota(jnp.int32, (BLOCK, BLOCK), 1)


def spread_kernel(weight, copies):
    for chip in range(copies.shape[0]):
        copies[chip] = weight[...]


def prepare_kernel(group, core, hidden, near, far, keep, *give):
    wide = 2 * HD
    at = lax.broadcasted_iota(jnp.int32, (wide, wide), 0)
    to = lax.broadcasted_iota(jnp.int32, (wide, wide), 1)
    parity = jnp.where(to < HD, core[0], 1 - core[0])
    slot = lax.rem(to, HD)
    source = (lax.div(slot, group) * CORES + parity) * group + lax.rem(slot, group)
    order = jnp.where(at == source, 1.0, 0.0).astype(BF16)
    for step in range(hidden.shape[1] // wide):
        columns = mxu(hidden[:, step * wide : (step + 1) * wide], order).astype(BF16)
        span = slice(step * HD, (step + 1) * HD)
        near[:, span] = columns[:, :HD]
        far[:, span] = columns[:, HD:]
        keep[span, :] = columns[:, :HD].T
        which, first = divmod(step * HD, give[0].shape[0])
        give[which][first : first + HD, :] = columns[:, HD:].T


def half_kernel(near, mine, partial):
    chips, group, columns = mine.shape
    for rows in chunks(near.shape[0]):
        partial[rows, :] = mxu(near[rows, :], mine[...].reshape(chips * group, columns))


def project_kernel(far, other, partial, cotangent, query, kv, parts, held, sems):
    chips, group, columns = other.shape
    stores = []
    for rows in chunks(far.shape[0]):
        weight = other[...].reshape(chips * group, columns)
        part = partial[rows, :] + mxu(far[rows, :], weight)
        held[rows, :] = part[:, :HD]
        kv[rows, :] = part[:, HD:]
        stores.append(
            pltpu.make_async_copy(held.at[rows, :], query.at[rows, :], sems.at[len(stores)])
        )
        stores[-1].start()
    kv_state = jnp.zeros((HD, HD), F32)
    qg_state = jnp.zeros((HD, HD), F32)
    for rows in chunks(far.shape[0]):
        kv_state += gram(beside(kv[rows, :HD]), beside(kv[rows, HD:]))
        qg_state += gram(beside(held[rows, :]), beside(cotangent[rows, :]))
    piece = HD // chips
    for chip in range(chips):
        parts[chip] = kv_state[chip * piece : (chip + 1) * piece]
        parts[chips + chip] = qg_state[chip * piece : (chip + 1) * piece]
    for store in stores:
        store.wait()


def local_kernel(query, kv, cotangent, dlocal, inner):
    mask = causal()
    order = chunks(query.shape[0])
    state = jnp.zeros((HD, HD), F32)
    for rows in order:
        keys, values = kv[rows, :HD], kv[rows, HD:]
        queries, cot = beside(query[rows, :]), beside(cotangent[rows, :])
        scores = jnp.where(mask, cross(queries, keys), 0.0)
        dmat = jnp.where(mask, cross(cot, values), 0.0)
        dquery = times(beside(dmat), doubled(keys))
        out = times(beside(scores), doubled(values))
        if rows is not order[0]:
            dquery += times(cot, doubled(state.T))
            out += times(queries, doubled(state))
        inner[rows, :] = out
        dlocal[rows, 0:HD] = dquery
        dlocal[rows, HD : 2 * HD] = gram(beside(dmat), queries)
        dlocal[rows, 2 * HD :] = gram(beside(scores), cot)
        if rows is not order[-1]:
            state += gram(beside(keys), beside(values))
    state = jnp.zeros((HD, HD), F32)
    for later, rows in zip(order[:0:-1], order[-2::-1]):
        state += gram(beside(query[later, :]), beside(cotangent[later, :]))
        dlocal[rows, HD : 2 * HD] += times(beside(kv[rows, HD:]), doubled(state.T))
        dlocal[rows, 2 * HD :] += times(beside(kv[rows, :HD]), doubled(state))


def scan_kernel(core, pieces, sums):
    devices = pieces.shape[0]
    flip = core[0] == 1
    total = jnp.zeros(pieces.shape[1:], F32)
    rank = [(slab % CORES) * (devices // CORES) + slab // CORES for slab in range(devices)]
    for step in range(devices):
        source = jnp.where(flip, rank[devices - 1 - step], rank[step])
        sums[source] = total
        total += pieces[source]


def joined(back, which, states):
    chips, piece = back.shape[0] // CORES, back.shape[1]
    for chip in range(chips):
        states[which, chip * piece : (chip + 1) * piece, :] = back[which * chips + chip]
    return states[which]


def dproj_kernel(scale, back, kv, cotangent, dlocal, dproj, states):
    before, after = joined(back, 0, states), joined(back, 1, states)
    prefix, suffix, turned = doubled(before.T), doubled(after), doubled(after.T)
    for rows in chunks(kv.shape[0]):
        for j, term in enumerate(
            (
                times(beside(cotangent[rows, :]), prefix),
                times(beside(kv[rows, HD:]), turned),
                times(beside(kv[rows, :HD]), suffix),
            )
        ):
            columns = slice(j * HD, (j + 1) * HD)
            dproj[rows, columns] = (scale * (dlocal[rows, columns] + term)).astype(BF16)


def attended_kernel(scale, back, query, inner, attended, states):
    prefix = doubled(joined(back, 0, states))
    for rows in chunks(query.shape[0]):
        attended[rows, :] = scale * (inner[rows, :] + times(beside(query[rows, :]), prefix))


def own_kernel(turned, dproj, *refs):
    taken, (product, held, sems) = refs[:PARTS], refs[PARTS:]
    size = taken[0].shape[0]
    loads = [
        pltpu.make_async_copy(part, held.at[index * size : (index + 1) * size, :], sems.at[index])
        for index, part in enumerate(taken)
    ]
    for load in loads:
        load.start()
    for rows in chunks(turned.shape[0]):
        product[rows, :] = mxu(turned[rows, :], dproj[...])
    for load in loads:
        load.wait()


def total_kernel(turned, dproj, product, total):
    for rows in chunks(turned.shape[0]):
        total[rows, :] = (product[rows, :] + mxu(turned[rows, :], dproj[...])).astype(BF16)


def sum_kernel(scale, landed, grad):
    total = landed[0].astype(F32)
    for chip in range(1, landed.shape[0]):
        total += landed[chip].astype(F32)
    grad[...] = scale * total


def local(hidden, qkv_weight, out_grad):
    tokens, width = hidden.shape
    group, columns = qkv_weight.shape
    chips = lax.axis_size("chip")
    devices = chips * CORES
    piece = HD // chips
    total_tokens = tokens * devices
    scale = float(HD * total_tokens) ** (-0.5)
    grad_scale = float(total_tokens) ** (-0.5)
    core = lax.axis_index("core").astype(jnp.int32).reshape(1)
    half = width // CORES
    square = tokens * HD * HD
    states = [pltpu.VMEM((2, HD, HD), F32)]

    (copies,) = call(
        spread_kernel, [vmem((chips, group, columns), BF16)], [qkv_weight], 1024, 8, [VMEM]
    )
    mine = lax.all_to_all(copies, "chip", 0, 0, tiled=True)
    near, far, keep, *give = call(
        functools.partial(prepare_kernel, group),
        [
            vmem((tokens, half), BF16),
            hbm((tokens, half), BF16),
            hbm((half, tokens), BF16),
        ]
        + [hbm((half // PARTS, tokens), BF16)] * PARTS,
        [core, hidden],
        tokens * width * 1024,
        24,
        [SMEM, VMEM],
    )
    taken = [lax.ppermute(part, "core", SWAP) for part in give]
    mine, near, far, keep, taken = lax.optimization_barrier((mine, near, far, keep, taken))
    other = lax.ppermute(mine, "core", SWAP)
    (partial,) = call(
        half_kernel,
        [vmem((tokens, columns))],
        [near, mine],
        2 * tokens * half * columns,
        16,
        [VMEM, VMEM],
    )
    query, kv, parts = call(
        project_kernel,
        [direct((tokens, HD)), vmem((tokens, 2 * HD)), vmem((devices, piece, HD))],
        [far, other, partial, out_grad],
        2 * tokens * half * columns + 16 * square,
        24,
        [VMEM] * 4,
        [pltpu.VMEM((tokens, HD), F32), pltpu.SemaphoreType.DMA((tokens // BLOCK,))],
    )
    pieces = lax.all_to_all(parts, RANKS, 0, 0, tiled=True)
    dlocal, inner = call(
        local_kernel,
        [vmem((tokens, columns)), hbm((tokens, HD))],
        [query, kv, out_grad],
        15 * 6 * square,
        24,
        [VMEM] * 3,
    )
    pieces, dlocal = lax.optimization_barrier((pieces, dlocal))
    (sums,) = call(
        scan_kernel, [vmem(parts.shape)], [core, pieces], devices * HD * HD, 8, [SMEM, VMEM]
    )
    back = lax.all_to_all(sums, RANKS, 0, 0, tiled=True)

    (dproj,) = call(
        functools.partial(dproj_kernel, scale),
        [vmem((tokens, columns), BF16)],
        [back, kv, out_grad, dlocal],
        24 * square,
        24,
        [VMEM] * 4,
        states,
    )
    theirs = lax.ppermute(dproj, "core", SWAP)
    product, held = call(
        own_kernel,
        [vmem((half, columns)), (pltpu.VMEM((half, tokens), BF16), VMEM)],
        [keep, dproj, *taken],
        2 * half * tokens * columns,
        24,
        [VMEM, VMEM] + [HBM] * PARTS,
        [pltpu.SemaphoreType.DMA((PARTS,))],
    )
    (attended,) = call(
        functools.partial(attended_kernel, scale),
        [hbm((tokens, HD))],
        [back, query, inner],
        4 * square,
        24,
        [VMEM] * 3,
        states,
    )
    product, held, attended = lax.optimization_barrier((product, held, attended))
    (total,) = call(
        total_kernel,
        [vmem((half, columns), BF16)],
        [held, theirs, product],
        2 * half * tokens * columns,
        24,
        [VMEM] * 3,
    )
    landed = lax.all_to_all(total.reshape(chips, group, columns), "chip", 0, 0, tiled=True)
    (grad,) = call(
        functools.partial(sum_kernel, grad_scale),
        [hbm((group, columns))],
        [landed],
        half * columns,
        16,
        [VMEM],
    )
    return attended, grad


def solution(mesh):
    chips, heads = mesh.shape["ctx"] // CORES, mesh.shape["head"]
    fine = Mesh(mesh.devices.reshape(chips, CORES, heads), ("chip", "core", "head"))
    return jax.shard_map(
        local,
        mesh=fine,
        in_specs=(P(CTX, None), P(CTX, "head"), P(CTX, "head")),
        out_specs=(P(CTX, "head"), P(CTX, "head")),
        check_vma=False,
    )
```

```python
import functools

import jax
import jax.numpy as jnp
from jax import lax
from jax.experimental import pallas as pl
from jax.experimental.pallas import tpu as pltpu
from jax.sharding import Mesh, PartitionSpec as P

HD = 128
BLOCK = 256
PARTS = 4
CORES = 2
MIB = 1 << 20

SWAP = [(0, 1), (1, 0)]
CTX = ("chip", "core")
RANKS = ("core", "chip")
F32 = jnp.float32
BF16 = jnp.bfloat16

PLAIN = (((1,), (0,)), ((), ()))
ROWS = (((1,), (1,)), ((), ()))
COLS = (((0,), (0,)), ((), ()))


def mxu(a, b, dims=PLAIN):
    return lax.dot_general(a, b, dims, preferred_element_type=F32)


def split(x):
    high = x.astype(BF16)
    return high, (x - high.astype(F32)).astype(BF16)


def beside(x):
    return jnp.concatenate(split(x), axis=1)


def doubled(x):
    both = beside(x)
    return jnp.concatenate([both, both], axis=0)


def folded(out):
    width = out.shape[1] // 2
    return out[:, :width] + out[:, width:]


def times(left, right):
    return folded(mxu(left, right))


def gram(left, right):
    out = folded(mxu(left, right, COLS))
    height = out.shape[0] // 2
    return out[:height] + out[height:]


def cross(left, right):
    high, low = split(right)
    return mxu(left, jnp.concatenate([high, high], axis=1), ROWS) + mxu(
        left, jnp.concatenate([low, low], axis=1), ROWS
    )


HBM = pl.BlockSpec(memory_space=pltpu.HBM)
VMEM = pl.BlockSpec(memory_space=pltpu.VMEM)
SMEM = pl.BlockSpec(memory_space=pltpu.SMEM)


def vmem(dims, dtype=F32):
    return jax.ShapeDtypeStruct(dims, dtype), VMEM


def hbm(dims, dtype=F32):
    return pltpu.HBM(dims, dtype), VMEM


def direct(dims, dtype=F32):
    return pltpu.HBM(dims, dtype), HBM


def call(body, outs, args, flops, limit, specs, scratch=()):
    size = sum(a.size * a.dtype.itemsize for a in args)
    args = [
        pltpu.with_memory_space_constraint(a, pltpu.HBM) if spec is HBM else a
        for a, spec in zip(args, specs)
    ]
    return pl.pallas_call(
        body,
        out_shape=[kind for kind, _ in outs],
        in_specs=specs,
        out_specs=[spec for _, spec in outs],
        scratch_shapes=list(scratch),
        cost_estimate=pl.CostEstimate(flops=flops, bytes_accessed=size, transcendentals=0),
        compiler_params=pltpu.CompilerParams(vmem_limit_bytes=limit * MIB),
    )(*args)


def chunks(total):
    return [slice(start, start + BLOCK) for start in range(0, total, BLOCK)]


def causal():
    at = lax.broadcasted_iota(jnp.int32, (BLOCK, BLOCK), 0)
    return at >= lax.broadcasted_iota(jnp.int32, (BLOCK, BLOCK), 1)


def spread_kernel(weight, copies):
    for chip in range(copies.shape[0]):
        copies[chip] = weight[...]


def prepare_kernel(group, core, hidden, near, far, keep, *give):
    wide = 2 * HD
    at = lax.broadcasted_iota(jnp.int32, (wide, wide), 0)
    to = lax.broadcasted_iota(jnp.int32, (wide, wide), 1)
    parity = jnp.where(to < HD, core[0], 1 - core[0])
    slot = lax.rem(to, HD)
    source = (lax.div(slot, group) * CORES + parity) * group + lax.rem(slot, group)
    order = jnp.where(at == source, 1.0, 0.0).astype(BF16)
    for step in range(hidden.shape[1] // wide):
        columns = mxu(hidden[:, step * wide : (step + 1) * wide], order).astype(BF16)
        span = slice(step * HD, (step + 1) * HD)
        near[:, span] = columns[:, :HD]
        far[:, span] = columns[:, HD:]
        keep[span, :] = columns[:, :HD].T
        which, first = divmod(step * HD, give[0].shape[0])
        give[which][first : first + HD, :] = columns[:, HD:].T


def half_kernel(near, mine, partial):
    chips, group, columns = mine.shape
    for rows in chunks(near.shape[0]):
        partial[rows, :] = mxu(near[rows, :], mine[...].reshape(chips * group, columns))


def project_kernel(far, other, partial, cotangent, query, kv, parts, held, sems):
    chips, group, columns = other.shape
    stores = []
    for rows in chunks(far.shape[0]):
        weight = other[...].reshape(chips * group, columns)
        part = partial[rows, :] + mxu(far[rows, :], weight)
        held[rows, :] = part[:, :HD]
        kv[rows, :] = part[:, HD:]
        stores.append(
            pltpu.make_async_copy(held.at[rows, :], query.at[rows, :], sems.at[len(stores)])
        )
        stores[-1].start()
    kv_state = jnp.zeros((HD, HD), F32)
    qg_state = jnp.zeros((HD, HD), F32)
    for rows in chunks(far.shape[0]):
        kv_state += gram(beside(kv[rows, :HD]), beside(kv[rows, HD:]))
        qg_state += gram(beside(held[rows, :]), beside(cotangent[rows, :]))
    piece = HD // chips
    for chip in range(chips):
        parts[chip] = kv_state[chip * piece : (chip + 1) * piece]
        parts[chips + chip] = qg_state[chip * piece : (chip + 1) * piece]
    for store in stores:
        store.wait()


def local_kernel(query, kv, cotangent, dlocal, inner):
    mask = causal()
    order = chunks(query.shape[0])
    state = jnp.zeros((HD, HD), F32)
    for rows in order:
        keys, values = kv[rows, :HD], kv[rows, HD:]
        queries, cot = beside(query[rows, :]), beside(cotangent[rows, :])
        scores = jnp.where(mask, cross(queries, keys), 0.0)
        dmat = jnp.where(mask, cross(cot, values), 0.0)
        dquery = times(beside(dmat), doubled(keys))
        out = times(beside(scores), doubled(values))
        if rows is not order[0]:
            dquery += times(cot, doubled(state.T))
            out += times(queries, doubled(state))
        inner[rows, :] = out
        dlocal[rows, 0:HD] = dquery
        dlocal[rows, HD : 2 * HD] = gram(beside(dmat), queries)
        dlocal[rows, 2 * HD :] = gram(beside(scores), cot)
        if rows is not order[-1]:
            state += gram(beside(keys), beside(values))
    state = jnp.zeros((HD, HD), F32)
    for later, rows in zip(order[:0:-1], order[-2::-1]):
        state += gram(beside(query[later, :]), beside(cotangent[later, :]))
        dlocal[rows, HD : 2 * HD] += times(beside(kv[rows, HD:]), doubled(state.T))
        dlocal[rows, 2 * HD :] += times(beside(kv[rows, :HD]), doubled(state))


def scan_kernel(core, pieces, sums):
    devices = pieces.shape[0]
    flip = core[0] == 1
    total = jnp.zeros(pieces.shape[1:], F32)
    rank = [(slab % CORES) * (devices // CORES) + slab // CORES for slab in range(devices)]
    for step in range(devices):
        source = jnp.where(flip, rank[devices - 1 - step], rank[step])
        sums[source] = total
        total += pieces[source]


def joined(back, which, states):
    chips, piece = back.shape[0] // CORES, back.shape[1]
    for chip in range(chips):
        states[which, chip * piece : (chip + 1) * piece, :] = back[which * chips + chip]
    return states[which]


def dproj_kernel(scale, back, kv, cotangent, dlocal, dproj, states):
    before, after = joined(back, 0, states), joined(back, 1, states)
    prefix, suffix, turned = doubled(before.T), doubled(after), doubled(after.T)
    for rows in chunks(kv.shape[0]):
        for j, term in enumerate(
            (
                times(beside(cotangent[rows, :]), prefix),
                times(beside(kv[rows, HD:]), turned),
                times(beside(kv[rows, :HD]), suffix),
            )
        ):
            columns = slice(j * HD, (j + 1) * HD)
            dproj[rows, columns] = (scale * (dlocal[rows, columns] + term)).astype(BF16)


def own_kernel(scale, turned, dproj, back, query, inner, *refs):
    taken, (product, held, attended, rows_out, states, sems, out_sems) = refs[:PARTS], refs[PARTS:]
    size = taken[0].shape[0]
    loads = [
        pltpu.make_async_copy(part, held.at[index * size : (index + 1) * size, :], sems.at[index])
        for index, part in enumerate(taken)
    ]
    for load in loads:
        load.start()
    prefix = doubled(joined(back, 0, states))
    stores = []
    for index, rows in enumerate(chunks(query.shape[0])):
        rows_out[rows, :] = scale * (inner[rows, :] + times(beside(query[rows, :]), prefix))
        stores.append(
            pltpu.make_async_copy(rows_out.at[rows, :], attended.at[rows, :], out_sems.at[index])
        )
        stores[-1].start()
    for rows in chunks(turned.shape[0]):
        product[rows, :] = mxu(turned[rows, :], dproj[...])
    for copy in loads + stores:
        copy.wait()


def total_kernel(turned, dproj, product, total):
    for rows in chunks(turned.shape[0]):
        total[rows, :] = (product[rows, :] + mxu(turned[rows, :], dproj[...])).astype(BF16)


def sum_kernel(scale, landed, grad):
    total = landed[0].astype(F32)
    for chip in range(1, landed.shape[0]):
        total += landed[chip].astype(F32)
    grad[...] = scale * total


def local(hidden, qkv_weight, out_grad):
    tokens, width = hidden.shape
    group, columns = qkv_weight.shape
    chips = lax.axis_size("chip")
    devices = chips * CORES
    piece = HD // chips
    total_tokens = tokens * devices
    scale = float(HD * total_tokens) ** (-0.5)
    grad_scale = float(total_tokens) ** (-0.5)
    core = lax.axis_index("core").astype(jnp.int32).reshape(1)
    half = width // CORES
    square = tokens * HD * HD
    states = [pltpu.VMEM((2, HD, HD), F32)]

    (copies,) = call(
        spread_kernel, [vmem((chips, group, columns), BF16)], [qkv_weight], 1024, 8, [VMEM]
    )
    mine = lax.all_to_all(copies, "chip", 0, 0, tiled=True)
    near, far, keep, *give = call(
        functools.partial(prepare_kernel, group),
        [
            vmem((tokens, half), BF16),
            hbm((tokens, half), BF16),
            hbm((half, tokens), BF16),
        ]
        + [hbm((half // PARTS, tokens), BF16)] * PARTS,
        [core, hidden],
        tokens * width * 1024,
        24,
        [SMEM, VMEM],
    )
    taken = [lax.ppermute(part, "core", SWAP) for part in give]
    mine, near, far, keep, taken = lax.optimization_barrier((mine, near, far, keep, taken))
    other = lax.ppermute(mine, "core", SWAP)
    (partial,) = call(
        half_kernel,
        [vmem((tokens, columns))],
        [near, mine],
        2 * tokens * half * columns,
        16,
        [VMEM, VMEM],
    )
    query, kv, parts = call(
        project_kernel,
        [direct((tokens, HD)), vmem((tokens, 2 * HD)), vmem((devices, piece, HD))],
        [far, other, partial, out_grad],
        2 * tokens * half * columns + 16 * square,
        24,
        [VMEM] * 4,
        [pltpu.VMEM((tokens, HD), F32), pltpu.SemaphoreType.DMA((tokens // BLOCK,))],
    )
    pieces = lax.all_to_all(parts, RANKS, 0, 0, tiled=True)
    dlocal, inner = call(
        local_kernel,
        [vmem((tokens, columns)), hbm((tokens, HD))],
        [query, kv, out_grad],
        15 * 6 * square,
        24,
        [VMEM] * 3,
    )
    pieces, dlocal = lax.optimization_barrier((pieces, dlocal))
    (sums,) = call(
        scan_kernel, [vmem(parts.shape)], [core, pieces], devices * HD * HD, 8, [SMEM, VMEM]
    )
    back = lax.all_to_all(sums, RANKS, 0, 0, tiled=True)

    (dproj,) = call(
        functools.partial(dproj_kernel, scale),
        [vmem((tokens, columns), BF16)],
        [back, kv, out_grad, dlocal],
        24 * square,
        24,
        [VMEM] * 4,
        states,
    )
    theirs = lax.ppermute(dproj, "core", SWAP)
    product, held, attended = call(
        functools.partial(own_kernel, scale),
        [
            vmem((half, columns)),
            (pltpu.VMEM((half, tokens), BF16), VMEM),
            direct((tokens, HD)),
        ],
        [keep, dproj, back, query, inner, *taken],
        2 * half * tokens * columns,
        24,
        [VMEM] * 5 + [HBM] * PARTS,
        [
            pltpu.VMEM((tokens, HD), F32),
            *states,
            pltpu.SemaphoreType.DMA((PARTS,)),
            pltpu.SemaphoreType.DMA((tokens // BLOCK,)),
        ],
    )
    (total,) = call(
        total_kernel,
        [vmem((half, columns), BF16)],
        [held, theirs, product],
        2 * half * tokens * columns,
        24,
        [VMEM] * 3,
    )
    landed = lax.all_to_all(total.reshape(chips, group, columns), "chip", 0, 0, tiled=True)
    (grad,) = call(
        functools.partial(sum_kernel, grad_scale),
        [hbm((group, columns))],
        [landed],
        half * columns,
        16,
        [VMEM],
    )
    return attended, grad


def solution(mesh):
    chips, heads = mesh.shape["ctx"] // CORES, mesh.shape["head"]
    fine = Mesh(mesh.devices.reshape(chips, CORES, heads), ("chip", "core", "head"))
    return jax.shard_map(
        local,
        mesh=fine,
        in_specs=(P(CTX, None), P(CTX, "head"), P(CTX, "head")),
        out_specs=(P(CTX, "head"), P(CTX, "head")),
        check_vma=False,
    )
```
